512 devices in a mesh: inst: 8 (over y), space: 64 (over x, z, core).
Axes of the slice: x: 4, y: 8, z: 8, core: 2. Of those that a mesh axis runs over, the one named last changes fastest.
Arguments:
- adjoint: float32 [16, 5, 8192, 128], P('inst', None, 'space'), may hold values from -6 to 6
- source: float32 [16, 5, 8192, 128], P('inst', None, 'space'), may hold values from -6 to 6
- coefficient: float32 [5, 8192, 128], P(None, 'space'), may hold values from 0.2 to 2
- volume: float32 [8192, 128], P('space'), may hold values from 0.5 to 2
- mixing: float32 [5, 5, 5], replicated, may hold values from -2.5 to 2.5
- face_partner: int32 [16, 256], P('inst'), may hold values from 0 to 255, as said below
Outputs:
- residual: float32 [16, 5, 8192, 128], P('inst', None, 'space')
The draws below stay inside these ranges and needn't reach their ends.
Inputs may be any that keep to these rules, and one draw needn't show every extreme that they name: `face_partner`: for each instance n there is a rotation s_n = 4 * k_n + e_n with k_n in 1 to 30 and e_n in 1 to 3. A global block x = 4 * p + b (sector j = p // 2) has index j * 4 + b within its blade row; a rotor block of index G is paired with the stator block of index (G + s_n) mod 128, a stator block of index G with the rotor block of index (G - s_n) mod 128; the partner of index H lies on device 2 * (H // 4) plus 1 for a stator partner, as block H mod 4.
All inputs are finite; a program needn't handle non-finite values.
Results may differ from the reference program's by a relative error of at most 0.000059.
Values sent between devices are 32-bit elements; how exact they have to be, the bound alone decides.
A program may use at most 64 MiB of HBM per device.

```python
import math
import jax
import jax.numpy as jnp
from jax import lax

NI = 16
NV = 5
CA = 128
NR = 128
NB = 4
FB = 32
NA = 8192
FACE_BLOCKS = 256
HALF_BLOCKS = 128


def draw_face_partner(key, part):
    key = jax.random.fold_in(key, 7)
    sector_key, block_key = jax.random.split(key)
    sector_count = HALF_BLOCKS // NB
    sector_part = jax.random.randint(sector_key, (NI, 1), 1, sector_count - 1)
    block_part = 1 + jax.random.randint(block_key, (NI, 1), 0, NB - 1)
    shift_blocks = sector_part * NB + block_part
    block_index = jnp.arange(FACE_BLOCKS)[None, :]
    device = block_index // NB
    sector_block = device // 2 * NB + block_index % NB
    face_side = device % 2
    moved_block = jnp.where(face_side == 0, sector_block + shift_blocks, sector_block - shift_blocks) % HALF_BLOCKS
    partner_device = 2 * (moved_block // NB) + 1 - face_side
    return (partner_device * NB + moved_block % NB).astype(jnp.int32)


def block_scale(own_key, extent, cuts, smallest, top_value):
    gain = 1.0
    for dim, parts in cuts:
        draws = jax.random.uniform(jax.random.fold_in(jax.random.fold_in(own_key, 6), dim), (parts,), jnp.float32, smallest / len(cuts), top_value / len(cuts))
        gain = gain * jnp.repeat(jnp.exp(draws), extent[dim] // parts).reshape((-1,) + (1,) * (len(extent) - 1 - dim))
    return gain


def centred(key, shape, deviation, reach, pieces=(), kind=jnp.bfloat16):
    factor_of = block_scale(key, shape, pieces, -0.22, 0.18) if pieces else 1.0
    result = jax.random.normal(key, shape, jnp.float32) * deviation * factor_of
    return jnp.minimum(jnp.maximum(result, -reach), reach).astype(kind)


def setup_inputs(seed: int = 0) -> dict:
    arg_keys = jax.random.split(jax.random.key(seed), 7)
    return {
        "adjoint": centred(arg_keys[0], (NI, NV, NA, NR), 1.0, 6.0, ((0, 8), (2, 64)), jnp.float32),
        "source": centred(arg_keys[1], (NI, NV, NA, NR), 1.0, 6.0, ((0, 8), (2, 64)), jnp.float32),
        "coefficient": jnp.clip(jnp.exp(math.log(2.0) - 2.3025851 * jax.random.uniform(arg_keys[2], (5, NA, NR), jnp.float32) ** block_scale(arg_keys[2], (5, NA, NR), ((1, 64),), -0.2, 0.2)), 0.2, 2.0),
        "volume": jnp.clip(jnp.exp(math.log(2.0) - 1.3862944 * jax.random.uniform(arg_keys[3], (NA, NR), jnp.float32) ** block_scale(arg_keys[3], (NA, NR), ((0, 64),), -0.2, 0.2)), 0.5, 2.0),
        "mixing": centred(arg_keys[4], (5, NV, NV), NV ** -0.5, 2.5, (), jnp.float32),
        "face_partner": draw_face_partner(jax.random.fold_in(arg_keys[6], 71), 0),
    }


highest = lax.Precision.HIGHEST
spin_rate = 0.75


def spectral_matrix(inst_count):
    inst_order = jnp.arange(inst_count)
    offset = inst_order[:, None] - inst_order[None, :]
    angle_value = jnp.pi * offset.astype(jnp.float32) / inst_count
    parity = jnp.where(offset % 2 == 0, 1.0, -1.0).astype(jnp.float32)
    sine_value = jnp.where(offset == 0, 1.0, jnp.sin(angle_value))
    return jnp.where(offset == 0, 0.0, 0.5 * parity * jnp.cos(angle_value) / sine_value).astype(jnp.float32)


def mix(matrix, grid_field):
    return jnp.einsum('uv,nuar->nvar', matrix, grid_field, precision=highest)


def roll_sides(grid_field, step_size):
    count_inst, count_var, count_rows, count_cells = grid_field.shape
    sectors = count_rows // (2 * CA)
    split_sides = grid_field.reshape(count_inst, count_var, sectors, 2, CA, count_cells).transpose(0, 1, 3, 2, 4, 5)
    rolled = jnp.roll(split_sides.reshape(count_inst, count_var, 2, sectors * CA, count_cells), step_size, axis=3)
    rolled = rolled.reshape(count_inst, count_var, 2, sectors, CA, count_cells).transpose(0, 1, 3, 2, 4, 5)
    return rolled.reshape(count_inst, count_var, count_rows, count_cells)


def reference(adjoint, source, coefficient, volume, mixing, face_partner):
    center = mix(mixing[0], coefficient[0][None, None] * adjoint)
    ahead_moved = roll_sides(coefficient[1][None, None] * adjoint, 1)
    behind_moved = roll_sides(coefficient[2][None, None] * adjoint, -1)
    outward = coefficient[3][None, None] * adjoint
    inward = coefficient[4][None, None] * adjoint
    face_rows = outward[:, :, :, NR - 1].reshape(NI, NV, FACE_BLOCKS, FB)
    picked = face_rows[jnp.arange(NI)[:, None], :, face_partner]
    received = picked.transpose(0, 2, 1, 3).reshape(NI, NV, NA)
    zero_column = jnp.zeros_like(outward[:, :, :, :1])
    radial_moved = jnp.concatenate([zero_column, outward[:, :, :, :-1]], axis=3).at[:, :, :, NR - 1].add(received)
    inward_moved = jnp.concatenate([inward[:, :, :, 1:], zero_column], axis=3)
    spectral = jnp.einsum('mn,mvar->nvar', spectral_matrix(NI), adjoint, precision=highest)
    total = source + center + mix(mixing[1], ahead_moved) + mix(mixing[2], behind_moved)
    total = total + mix(mixing[3], radial_moved) + mix(mixing[4], inward_moved)
    return total + spin_rate * volume[None, None] * spectral
```

```python
import functools

import numpy as np

import jax
import jax.numpy as jnp
from jax import lax
from jax.experimental import pallas as pl
from jax.experimental.pallas import tpu as pltpu
from jax.sharding import PartitionSpec as P

MESH = pl.DeviceIdType.MESH
NI = 16
ND = 8
NV = 5
NB = 4
FB = 32
BLK = 16
ROWS = 128
LANES = 128
SPIN_RATE = 0.75
CHUNKS = ((0, 3), (3, 2))
ORDER = (4, 3, 5, 2, 6, 1, 7)
VMEM_LIMIT = 48 * 1024 * 1024


def spectral_entries():
    offset = np.arange(1, NI)
    angle = np.pi * offset / NI
    entries = 0.5 * np.where(offset % 2 == 0, 1.0, -1.0) * np.cos(angle) / np.sin(angle)
    return np.concatenate([[0.0], entries])


def payload_kernel(adj, coef, out):
    lane = lax.broadcasted_iota(jnp.int32, (ROWS, LANES), 1)
    faces = jnp.zeros((ROWS, LANES), jnp.float32)
    outward = coef[3]
    for k in range(2 * NV):
        n, u = divmod(k, NV)
        moved = pltpu.roll(outward * adj[n, u], k + 1, 1)
        faces = jnp.where(lane == k, moved, faces)
    out[0:16, :] = faces.T[0:16, :]
    for k in range(2 * NV):
        n, u = divmod(k, NV)
        out[10 + k : 11 + k, :] = coef[1, ROWS - 1 : ROWS, :] * adj[n, u, ROWS - 1 : ROWS, :]
        out[20 + k : 21 + k, :] = coef[2, 0:1, :] * adj[n, u, 0:1, :]
    out[30:32, :] = jnp.zeros((2, LANES), jnp.float32)


def main_kernel(
    adj_hbm, src_hbm, coef_hbm, vol_hbm, mixing, _, out_hbm,
    adj, base, coef, vol, ahead, behind, gathered, turned, spectral,
    load_sem, store_sem, send1, recv1, send2, recv2,
):
    me = lax.axis_index("inst")
    barrier = pltpu.get_barrier_semaphore()
    for d in range(1, ND):
        pl.semaphore_signal(barrier, inc=1, device_id={"inst": lax.rem(me + d, ND)}, device_id_type=MESH)
    loads = [
        pltpu.make_async_copy(s, t, load_sem.at[i])
        for i, (s, t) in enumerate(((adj_hbm, adj), (coef_hbm, coef), (src_hbm, base), (vol_hbm, vol)))
    ]
    for copy in loads:
        copy.start()
    pl.semaphore_wait(barrier, ND - 1)

    my_rows = pl.ds(pl.multiple_of(me * BLK, BLK), BLK)

    def first(c, d):
        v0, nv = CHUNKS[c]
        to = lax.rem(me + d, ND)
        return pltpu.make_async_remote_copy(
            src_ref=adj_hbm.at[:, pl.ds(v0, nv), pl.ds(pl.multiple_of(to * BLK, BLK), BLK)],
            dst_ref=gathered.at[d, :, pl.ds(v0, nv)],
            send_sem=send1.at[c, d], recv_sem=recv1.at[c, d],
            device_id={"inst": to}, device_id_type=MESH,
        )

    def second(c, d):
        v0, nv = CHUNKS[c]
        to = lax.rem(me + d, ND)
        return pltpu.make_async_remote_copy(
            src_ref=turned.at[d, :, pl.ds(v0, nv)],
            dst_ref=spectral.at[:, pl.ds(v0, nv), my_rows],
            send_sem=send2.at[c, d], recv_sem=recv2.at[c, d],
            device_id={"inst": to}, device_id_type=MESH,
        )

    chunks = range(len(CHUNKS))
    for c in chunks:
        for d in ORDER:
            first(c, d).start()
    for copy in loads:
        copy.wait()

    lane = lax.broadcasted_iota(jnp.int32, (BLK, LANES), 1)

    def stencil(step, carry):
        n = step // (ROWS // BLK)
        rows = pl.ds(pl.multiple_of(lax.rem(step, ROWS // BLK) * BLK, BLK), BLK)
        field = [adj[n, u, rows, :] for u in range(NV)]
        total = [base[n, v, rows, :] for v in range(NV)]
        for k in range(5):
            scale = coef[k, rows, :]
            q = [scale * f for f in field]
            for v in range(NV):
                mixed = mixing[k, 0, v] * q[0]
                for u in range(1, NV):
                    mixed = mixed + mixing[k, u, v] * q[u]
                if k == 0:
                    total[v] = total[v] + mixed
                elif k == 1:
                    ahead[n, v, rows, :] = mixed
                elif k == 2:
                    behind[n, v, rows, :] = mixed
                elif k == 3:
                    total[v] = total[v] + jnp.where(lane == 0, 0.0, pltpu.roll(mixed, 1, 1))
                else:
                    total[v] = total[v] + jnp.where(lane == LANES - 1, 0.0, pltpu.roll(mixed, LANES - 1, 1))
        for v in range(NV):
            base[n, v, rows, :] = total[v]
        return carry

    lax.fori_loop(0, 2 * (ROWS // BLK), stencil, 0)

    row = lax.broadcasted_iota(jnp.int32, (ROWS, LANES), 0)

    def moved(step, carry):
        n, v = step // NV, lax.rem(step, NV)
        down = jnp.where(row == 0, 0.0, pltpu.roll(ahead[n, v], 1, 0))
        up = jnp.where(row == ROWS - 1, 0.0, pltpu.roll(behind[n, v], ROWS - 1, 0))
        base[n, v] = base[n, v] + (down + up)
        return carry

    lax.fori_loop(0, 2 * NV, moved, 0)

    entries = spectral_entries()
    half = NI // 2

    def transform(c):
        v0, nv = CHUNKS[c]

        def body(step, carry):
            v = v0 + step // 2
            part = lax.rem(step, 2) * 8
            rows = pl.ds(pl.multiple_of(part, 8), 8)
            mine = pl.ds(pl.multiple_of(me * BLK + part, 8), 8)
            x = []
            for a in range(NI):
                slot, i = (-(a // 2)) % ND, a % 2
                x.append(adj[i, v, mine, :] if slot == 0 else gathered[slot, i, v, rows, :])
            plus = [x[a] + x[a + half] for a in range(half)]
            minus = [x[a] - x[a + half] for a in range(half)]
            for b in range(half):
                even, odd = None, None
                for a in range(half):
                    low, high = entries[(a - b) % NI], entries[(a + half - b) % NI]
                    even_term = np.float32(0.5 * (low + high)) * plus[a]
                    odd_term = np.float32(0.5 * (low - high)) * minus[a]
                    even = even_term if even is None else even + even_term
                    odd = odd_term if odd is None else odd + odd_term
                for n, value in ((b, even + odd), (b + half, even - odd)):
                    slot, j = n // 2, n % 2
                    if slot == 0:
                        spectral[j, v, mine, :] = value
                    else:
                        turned[slot, j, v, rows, :] = value
            return carry

        lax.fori_loop(0, 2 * nv, body, 0)

    for c in chunks:
        for d in ORDER:
            first(c, d).wait_recv()
        transform(c)
        for d in ORDER:
            second(c, d).start()

    stores = []
    for c in chunks:
        v0, nv = CHUNKS[c]
        for d in ORDER:
            second(c, d).wait_recv()

        def finish(step, carry, v0=v0):
            v = v0 + step // 2
            n = lax.rem(step, 2)
            base[n, v] = base[n, v] + (SPIN_RATE * vol[...]) * spectral[n, v]
            return carry

        lax.fori_loop(0, 2 * nv, finish, 0)
        store = pltpu.make_async_copy(
            base.at[:, pl.ds(v0, nv)], out_hbm.at[:, pl.ds(v0, nv)], store_sem.at[c]
        )
        store.start()
        stores.append(store)
    for c in chunks:
        for d in ORDER:
            first(c, d).wait_send()
            second(c, d).wait_send()
    for store in stores:
        store.wait()


def last_kernel(part, received, mixing, partner, out, halo, face, sems):
    p = lax.axis_index("space")
    count = 64
    copies = [
        pltpu.make_async_copy(received.at[lax.rem(p + count - 2, count)], halo.at[0], sems.at[8]),
        pltpu.make_async_copy(received.at[lax.rem(p + 2, count)], halo.at[1], sems.at[9]),
    ]
    shifts = []
    for n in range(2):
        for b in range(NB):
            x = partner[n, NB * p + b]
            shifts.append(lax.rem(b - lax.rem(x, NB) + NB, NB) * FB)
            copies.append(
                pltpu.make_async_copy(received.at[x // NB, pl.ds(0, 16)], face.at[n * NB + b], sems.at[n * NB + b])
            )
    for copy in copies:
        copy.start()
    for copy in copies:
        copy.wait()
    lane = lax.broadcasted_iota(jnp.int32, (16, LANES), 1)
    mixed = []
    for n in range(2):
        rows = jnp.zeros((16, LANES), jnp.float32)
        for b in range(NB):
            rows = jnp.where(lane // FB == b, pltpu.roll(face[n * NB + b], shifts[n * NB + b], 1), rows)
        for v in range(NV):
            mixed.append(sum(mixing[3, u, v] * rows[n * NV + u : n * NV + u + 1, :] for u in range(NV)))
    mixed = jnp.concatenate(mixed + [jnp.zeros((LANES - 2 * NV, LANES), jnp.float32)], axis=0).T
    wide = lax.broadcasted_iota(jnp.int32, (ROWS, LANES), 1)
    for k in range(2 * NV):
        n, v = divmod(k, NV)
        column = pltpu.roll(mixed, LANES - 1 - k, 1)
        out[n, v] = part[n, v] + jnp.where(wide == LANES - 1, column, 0.0)
        first = sum(mixing[1, u, v] * halo[0, 10 + n * NV + u : 11 + n * NV + u, :] for u in range(NV))
        last = sum(mixing[2, u, v] * halo[1, 20 + n * NV + u : 21 + n * NV + u, :] for u in range(NV))
        out[n, v, 0:1, :] = out[n, v, 0:1, :] + first
        out[n, v, ROWS - 1 : ROWS, :] = out[n, v, ROWS - 1 : ROWS, :] + last


def local(adjoint, source, coefficient, volume, mixing, face_partner):
    f32 = jnp.float32
    vmem, smem, anywhere = (pl.BlockSpec(memory_space=s) for s in (pltpu.VMEM, pltpu.SMEM, pl.ANY))
    payload = pl.pallas_call(
        payload_kernel,
        out_shape=jax.ShapeDtypeStruct((32, LANES), f32),
        in_specs=[vmem, vmem],
        out_specs=vmem,
        name="payload",
    )(adjoint, coefficient)
    received = lax.all_gather(payload, "space")
    shard = (2, NV, ROWS, LANES)
    nc = len(CHUNKS)
    part = pl.pallas_call(
        main_kernel,
        out_shape=jax.ShapeDtypeStruct(shard, f32),
        in_specs=[anywhere, anywhere, anywhere, anywhere, smem, anywhere],
        out_specs=anywhere,
        scratch_shapes=[
            pltpu.VMEM(shard, f32), pltpu.VMEM(shard, f32),
            pltpu.VMEM((5, ROWS, LANES), f32), pltpu.VMEM((ROWS, LANES), f32),
            pltpu.VMEM(shard, f32), pltpu.VMEM(shard, f32),
            pltpu.VMEM((ND, 2, NV, BLK, LANES), f32), pltpu.VMEM((ND, 2, NV, BLK, LANES), f32),
            pltpu.VMEM(shard, f32),
            pltpu.SemaphoreType.DMA((4,)), pltpu.SemaphoreType.DMA((nc,)),
            pltpu.SemaphoreType.DMA((nc, ND)), pltpu.SemaphoreType.DMA((nc, ND)),
            pltpu.SemaphoreType.DMA((nc, ND)), pltpu.SemaphoreType.DMA((nc, ND)),
        ],
        compiler_params=pltpu.CompilerParams(
            collective_id=0, has_side_effects=True, vmem_limit_bytes=VMEM_LIMIT
        ),
        cost_estimate=pl.CostEstimate(flops=20_000_000, bytes_accessed=60_000_000, transcendentals=0),
        name="spectral_and_stencil",
    )(adjoint, source, coefficient, volume, mixing, payload)
    return pl.pallas_call(
        last_kernel,
        out_shape=jax.ShapeDtypeStruct(shard, f32),
        in_specs=[vmem, anywhere, smem, smem],
        out_specs=vmem,
        scratch_shapes=[
            pltpu.VMEM((2, 32, LANES), f32), pltpu.VMEM((2 * NB, 16, LANES), f32),
            pltpu.SemaphoreType.DMA((10,)),
        ],
        name="boundaries",
    )(part, received, mixing, face_partner)


def solution(mesh):
    in_specs = (
        P("inst", None, "space", None),
        P("inst", None, "space", None),
        P(None, "space", None),
        P("space", None),
        P(),
        P("inst", None),
    )
    out_specs = P("inst", None, "space", None)
    return jax.shard_map(local, mesh=mesh, in_specs=in_specs, out_specs=out_specs, check_vma=False)
```

```python
import functools

import numpy as np

import jax
import jax.numpy as jnp
from jax import lax
from jax.experimental import pallas as pl
from jax.experimental.pallas import tpu as pltpu
from jax.sharding import PartitionSpec as P

MESH = pl.DeviceIdType.MESH
NI = 16
ND = 8
NX = 4
NZ = 8
SECTORS = NX * NZ
SPACE = 2 * SECTORS
NV = 5
NB = 4
FB = 32
BLK = 16
ROWS = 128
LANES = 128
SPIN_RATE = 0.75
CHUNKS = ((0, 3), (3, 2))
ORDER = (4, 3, 5, 2, 6, 1, 7)
VMEM_LIMIT = 56 * 1024 * 1024


def spectral_entries():
    offset = np.arange(1, NI)
    angle = np.pi * offset / NI
    entries = 0.5 * np.where(offset % 2 == 0, 1.0, -1.0) * np.cos(angle) / np.sin(angle)
    return np.concatenate([[0.0], entries])


def main_kernel(
    adj_hbm, src_hbm, coef_hbm, vol_hbm, mixing, partner, out_hbm,
    adj, base, coef, vol, ahead, behind, gathered, turned, spectral, payload, faces, edges, halos,
    load_sem, store_sem, send1, recv1, send2, recv2, face_send, face_recv, halo_send, halo_recv,
):
    me = lax.axis_index("inst")
    p = lax.axis_index("space")
    side = lax.rem(p, 2)
    z, x = lax.rem(p // 2, NZ), p // (2 * NZ)
    rank = z * NX + x
    earlier = rank + 1 - side
    next_earlier, prev_earlier = z == NZ - 1, z != 0
    next_id = {"space": lax.rem(p + 2, SPACE)}
    prev_id = {"space": lax.rem(p + SPACE - 2, SPACE)}

    def across(r):
        return {"space": 2 * (lax.rem(r, NX) * NZ + r // NX) + 1 - side}

    barrier = pltpu.get_barrier_semaphore()

    def greet(device):
        pl.semaphore_signal(barrier, inc=1, device_id=device, device_id_type=MESH)

    for d in range(1, ND):
        greet({"inst": lax.rem(me + d, ND)})

    def greet_across(r, carry):
        greet(across(r))
        return carry

    lax.fori_loop(earlier, SECTORS, greet_across, 0)
    pl.when(jnp.logical_not(next_earlier))(lambda: greet(next_id))
    pl.when(jnp.logical_not(prev_earlier))(lambda: greet(prev_id))
    loads = [
        pltpu.make_async_copy(s, t, load_sem.at[i])
        for i, (s, t) in enumerate(((adj_hbm, adj), (coef_hbm, coef), (src_hbm, base), (vol_hbm, vol)))
    ]
    for copy in loads:
        copy.start()
    pl.semaphore_wait(barrier, ND - 1 + earlier + next_earlier.astype(jnp.int32) + prev_earlier.astype(jnp.int32))

    my_rows = pl.ds(pl.multiple_of(me * BLK, BLK), BLK)

    def first(c, d):
        v0, nv = CHUNKS[c]
        to = lax.rem(me + d, ND)
        return pltpu.make_async_remote_copy(
            src_ref=adj_hbm.at[:, pl.ds(v0, nv), pl.ds(pl.multiple_of(to * BLK, BLK), BLK)],
            dst_ref=gathered.at[d, :, pl.ds(v0, nv)],
            send_sem=send1.at[c, d], recv_sem=recv1.at[c, d],
            device_id={"inst": to}, device_id_type=MESH,
        )

    def second(c, d):
        v0, nv = CHUNKS[c]
        to = lax.rem(me + d, ND)
        return pltpu.make_async_remote_copy(
            src_ref=turned.at[d, :, pl.ds(v0, nv)],
            dst_ref=spectral.at[:, pl.ds(v0, nv), my_rows],
            send_sem=send2.at[c, d], recv_sem=recv2.at[c, d],
            device_id={"inst": to}, device_id_type=MESH,
        )

    def face_to(r):
        return pltpu.make_async_remote_copy(
            src_ref=payload, dst_ref=faces.at[rank],
            send_sem=face_send.at[r], recv_sem=face_recv.at[rank],
            device_id=across(r), device_id_type=MESH,
        )

    def face_from(r):
        return pltpu.make_async_remote_copy(
            src_ref=payload, dst_ref=faces.at[r],
            send_sem=face_send.at[r], recv_sem=face_recv.at[r],
            device_id=across(r), device_id_type=MESH,
        )

    def halo_to(i):
        return pltpu.make_async_remote_copy(
            src_ref=edges.at[i], dst_ref=halos.at[i],
            send_sem=halo_send.at[i], recv_sem=halo_recv.at[i],
            device_id=(next_id, prev_id)[i], device_id_type=MESH,
        )

    chunks = range(len(CHUNKS))
    for c in chunks:
        for d in ORDER:
            first(c, d).start()
    for copy in loads:
        copy.wait()

    wide = lax.broadcasted_iota(jnp.int32, (ROWS, LANES), 1)
    outward = coef[3]
    columns = jnp.zeros((ROWS, LANES), jnp.float32)
    for k in range(2 * NV):
        n, u = divmod(k, NV)
        columns = jnp.where(wide == k, pltpu.roll(outward * adj[n, u], k + 1, 1), columns)
        edges[0, k : k + 1, :] = coef[1, ROWS - 1 : ROWS, :] * adj[n, u, ROWS - 1 : ROWS, :]
        edges[1, k : k + 1, :] = coef[2, 0:1, :] * adj[n, u, 0:1, :]
    payload[...] = columns.T[0:16, :]
    for i in range(2):
        edges[i, 2 * NV : 16, :] = jnp.zeros((16 - 2 * NV, LANES), jnp.float32)

    def send_across(r, carry):
        face_to(r).start()
        return carry

    lax.fori_loop(0, earlier, send_across, 0)
    pl.when(next_earlier)(lambda: halo_to(0).start())
    pl.when(prev_earlier)(lambda: halo_to(1).start())

    lane = lax.broadcasted_iota(jnp.int32, (BLK, LANES), 1)

    def stencil(step, carry):
        n = step // (ROWS // BLK)
        rows = pl.ds(pl.multiple_of(lax.rem(step, ROWS // BLK) * BLK, BLK), BLK)
        field = [adj[n, u, rows, :] for u in range(NV)]
        total = [base[n, v, rows, :] for v in range(NV)]
        for k in range(5):
            scale = coef[k, rows, :]
            q = [scale * f for f in field]
            for v in range(NV):
                mixed = mixing[k, 0, v] * q[0]
                for u in range(1, NV):
                    mixed = mixed + mixing[k, u, v] * q[u]
                if k == 0:
                    total[v] = total[v] + mixed
                elif k == 1:
                    ahead[n, v, rows, :] = mixed
                elif k == 2:
                    behind[n, v, rows, :] = mixed
                elif k == 3:
                    total[v] = total[v] + jnp.where(lane == 0, 0.0, pltpu.roll(mixed, 1, 1))
                else:
                    total[v] = total[v] + jnp.where(lane == LANES - 1, 0.0, pltpu.roll(mixed, LANES - 1, 1))
        for v in range(NV):
            base[n, v, rows, :] = total[v]
        return carry

    lax.fori_loop(0, 2 * (ROWS // BLK), stencil, 0)

    row = lax.broadcasted_iota(jnp.int32, (ROWS, LANES), 0)

    def moved(step, carry):
        n, v = step // NV, lax.rem(step, NV)
        down = jnp.where(row == 0, 0.0, pltpu.roll(ahead[n, v], 1, 0))
        up = jnp.where(row == ROWS - 1, 0.0, pltpu.roll(behind[n, v], ROWS - 1, 0))
        base[n, v] = base[n, v] + (down + up)
        return carry

    lax.fori_loop(0, 2 * NV, moved, 0)

    entries = spectral_entries()
    half = NI // 2

    def transform(c):
        v0, nv = CHUNKS[c]

        def body(step, carry):
            v = v0 + step // 2
            part = lax.rem(step, 2) * 8
            rows = pl.ds(pl.multiple_of(part, 8), 8)
            mine = pl.ds(pl.multiple_of(me * BLK + part, 8), 8)
            x = []
            for a in range(NI):
                slot, i = (-(a // 2)) % ND, a % 2
                x.append(adj[i, v, mine, :] if slot == 0 else gathered[slot, i, v, rows, :])
            plus = [x[a] + x[a + half] for a in range(half)]
            minus = [x[a] - x[a + half] for a in range(half)]
            for b in range(half):
                even, odd = None, None
                for a in range(half):
                    low, high = entries[(a - b) % NI], entries[(a + half - b) % NI]
                    even_term = np.float32(0.5 * (low + high)) * plus[a]
                    odd_term = np.float32(0.5 * (low - high)) * minus[a]
                    even = even_term if even is None else even + even_term
                    odd = odd_term if odd is None else odd + odd_term
                for n, value in ((b, even + odd), (b + half, even - odd)):
                    slot, j = n // 2, n % 2
                    if slot == 0:
                        spectral[j, v, mine, :] = value
                    else:
                        turned[slot, j, v, rows, :] = value
            return carry

        lax.fori_loop(0, 2 * nv, body, 0)

    for c in chunks:
        for d in ORDER:
            first(c, d).wait_recv()
        transform(c)
        for d in ORDER:
            second(c, d).start()

    def answer_across(r, carry):
        face_from(r).wait_recv()
        face_to(r).start()
        return carry

    def answer_next():
        halo_to(1).wait_recv()
        halo_to(0).start()

    def answer_prev():
        halo_to(0).wait_recv()
        halo_to(1).start()

    pl.when(jnp.logical_not(next_earlier))(answer_next)
    pl.when(jnp.logical_not(prev_earlier))(answer_prev)
    lax.fori_loop(earlier, SECTORS, answer_across, 0)

    def take_across(r, carry):
        face_from(r).wait_recv()
        return carry

    pl.when(next_earlier)(lambda: halo_to(1).wait_recv())
    pl.when(prev_earlier)(lambda: halo_to(0).wait_recv())
    lax.fori_loop(0, earlier, take_across, 0)

    thin = lax.broadcasted_iota(jnp.int32, (16, LANES), 1) // FB
    mixed = []
    for n in range(2):
        rows = jnp.zeros((16, LANES), jnp.float32)
        for b in range(NB):
            block = partner[n, NB * p + b]
            sector, kind = block // (2 * NB), lax.rem(block, NB)
            face = faces[lax.rem(sector, NZ) * NX + sector // NZ]
            for turn in range(NB):
                here = jnp.logical_and(thin == b, kind == (b - turn) % NB)
                rows = jnp.where(here, pltpu.roll(face, turn * FB, 1) if turn else face, rows)
        for v in range(NV):
            mixed.append(sum(mixing[3, u, v] * rows[n * NV + u : n * NV + u + 1, :] for u in range(NV)))
    mixed = jnp.concatenate(mixed + [jnp.zeros((LANES - 2 * NV, LANES), jnp.float32)], axis=0).T
    for k in range(2 * NV):
        n, v = divmod(k, NV)
        column = pltpu.roll(mixed, LANES - 1 - k, 1)
        base[n, v] = base[n, v] + jnp.where(wide == LANES - 1, column, 0.0)
        first_row = sum(mixing[1, u, v] * halos[0, n * NV + u : n * NV + u + 1, :] for u in range(NV))
        last_row = sum(mixing[2, u, v] * halos[1, n * NV + u : n * NV + u + 1, :] for u in range(NV))
        base[n, v, 0:1, :] = base[n, v, 0:1, :] + first_row
        base[n, v, ROWS - 1 : ROWS, :] = base[n, v, ROWS - 1 : ROWS, :] + last_row

    stores = []
    for c in chunks:
        v0, nv = CHUNKS[c]
        for d in ORDER:
            second(c, d).wait_recv()

        def finish(step, carry, v0=v0):
            v = v0 + step // 2
            n = lax.rem(step, 2)
            base[n, v] = base[n, v] + (SPIN_RATE * vol[...]) * spectral[n, v]
            return carry

        lax.fori_loop(0, 2 * nv, finish, 0)
        store = pltpu.make_async_copy(
            base.at[:, pl.ds(v0, nv)], out_hbm.at[:, pl.ds(v0, nv)], store_sem.at[c]
        )
        store.start()
        stores.append(store)
    for c in chunks:
        for d in ORDER:
            first(c, d).wait_send()
            second(c, d).wait_send()

    def sent_across(r, carry):
        face_to(r).wait_send()
        return carry

    lax.fori_loop(0, SECTORS, sent_across, 0)
    for i in range(2):
        halo_to(i).wait_send()
    for store in stores:
        store.wait()


def local(adjoint, source, coefficient, volume, mixing, face_partner):
    f32 = jnp.float32
    smem, hbm = pl.BlockSpec(memory_space=pltpu.SMEM), pl.BlockSpec(memory_space=pltpu.HBM)
    shard = (2, NV, ROWS, LANES)
    nc = len(CHUNKS)
    return pl.pallas_call(
        main_kernel,
        out_shape=jax.ShapeDtypeStruct(shard, f32),
        in_specs=[hbm, hbm, hbm, hbm, smem, smem],
        out_specs=hbm,
        scratch_shapes=[
            pltpu.VMEM(shard, f32), pltpu.VMEM(shard, f32),
            pltpu.VMEM((5, ROWS, LANES), f32), pltpu.VMEM((ROWS, LANES), f32),
            pltpu.VMEM(shard, f32), pltpu.VMEM(shard, f32),
            pltpu.VMEM((ND, 2, NV, BLK, LANES), f32), pltpu.VMEM((ND, 2, NV, BLK, LANES), f32),
            pltpu.VMEM(shard, f32),
            pltpu.VMEM((16, LANES), f32), pltpu.VMEM((SECTORS, 16, LANES), f32),
            pltpu.VMEM((2, 16, LANES), f32), pltpu.VMEM((2, 16, LANES), f32),
            pltpu.SemaphoreType.DMA((4,)), pltpu.SemaphoreType.DMA((nc,)),
            pltpu.SemaphoreType.DMA((nc, ND)), pltpu.SemaphoreType.DMA((nc, ND)),
            pltpu.SemaphoreType.DMA((nc, ND)), pltpu.SemaphoreType.DMA((nc, ND)),
            pltpu.SemaphoreType.DMA((SECTORS,)), pltpu.SemaphoreType.DMA((SECTORS,)),
            pltpu.SemaphoreType.DMA((2,)), pltpu.SemaphoreType.DMA((2,)),
        ],
        compiler_params=pltpu.CompilerParams(
            collective_id=0, has_side_effects=True, vmem_limit_bytes=VMEM_LIMIT
        ),
        cost_estimate=pl.CostEstimate(flops=20_000_000, bytes_accessed=60_000_000, transcendentals=0),
        name="residual",
    )(adjoint, source, coefficient, volume, mixing, face_partner)


def solution(mesh):
    in_specs = (
        P("inst", None, "space", None),
        P("inst", None, "space", None),
        P(None, "space", None),
        P("space", None),
        P(),
        P("inst", None),
    )
    out_specs = P("inst", None, "space", None)
    return jax.shard_map(local, mesh=mesh, in_specs=in_specs, out_specs=out_specs, check_vma=False)
```

```python
import functools

import numpy as np

import jax
import jax.numpy as jnp
from jax import lax
from jax.experimental import pallas as pl
from jax.experimental.pallas import tpu as pltpu
from jax.sharding import PartitionSpec as P

MESH = pl.DeviceIdType.MESH
NI = 16
ND = 8
NX = 4
NZ = 8
SECTORS = NX * NZ
SPACE = 2 * SECTORS
NV = 5
NB = 4
FB = 32
BLK = 16
ROWS = 128
LANES = 128
SPIN_RATE = 0.75
CHUNKS = ((0, 3), (3, 2))
ORDER = (4, 3, 5, 2, 6, 1, 7)
VMEM_LIMIT = 16 * 1024 * 1024


def spectral_entries():
    offset = np.arange(1, NI)
    angle = np.pi * offset / NI
    entries = 0.5 * np.where(offset % 2 == 0, 1.0, -1.0) * np.cos(angle) / np.sin(angle)
    return np.concatenate([[0.0], entries])


def main_kernel(
    adj_hbm, src_hbm, coef_hbm, vol_hbm, mixing_hbm, partner_hbm, out_hbm,
    adj, base, coef, vol, ahead, behind, gathered, turned, spectral, payload, faces, edges, halos,
    mixing, partner,
    load_sem, store_sem, send1, recv1, send2, recv2, face_send, face_recv, halo_send, halo_recv,
):
    me = lax.axis_index("inst")
    p = lax.axis_index("space")
    side = lax.rem(p, 2)
    z, x = lax.rem(p // 2, NZ), p // (2 * NZ)
    rank = z * NX + x
    earlier = rank + 1 - side
    next_earlier, prev_earlier = z == NZ - 1, z != 0
    next_id = {"space": lax.rem(p + 2, SPACE)}
    prev_id = {"space": lax.rem(p + SPACE - 2, SPACE)}

    def across(r):
        return {"space": 2 * (lax.rem(r, NX) * NZ + r // NX) + 1 - side}

    barrier = pltpu.get_barrier_semaphore()

    def greet(device):
        pl.semaphore_signal(barrier, inc=1, device_id=device, device_id_type=MESH)

    for d in range(1, ND):
        greet({"inst": lax.rem(me + d, ND)})

    def greet_across(r, carry):
        greet(across(r))
        return carry

    lax.fori_loop(earlier, SECTORS, greet_across, 0)
    pl.when(jnp.logical_not(next_earlier))(lambda: greet(next_id))
    pl.when(jnp.logical_not(prev_earlier))(lambda: greet(prev_id))
    loads = [
        pltpu.make_async_copy(s, t, load_sem.at[i])
        for i, (s, t) in enumerate((
            (adj_hbm, adj), (coef_hbm, coef), (src_hbm, base), (vol_hbm, vol),
            (mixing_hbm, mixing), (partner_hbm, partner),
        ))
    ]
    for copy in loads:
        copy.start()
    pl.semaphore_wait(barrier, ND - 1 + earlier + next_earlier.astype(jnp.int32) + prev_earlier.astype(jnp.int32))

    my_rows = pl.ds(pl.multiple_of(me * BLK, BLK), BLK)

    def first(c, d):
        v0, nv = CHUNKS[c]
        to = lax.rem(me + d, ND)
        return pltpu.make_async_remote_copy(
            src_ref=adj_hbm.at[:, pl.ds(v0, nv), pl.ds(pl.multiple_of(to * BLK, BLK), BLK)],
            dst_ref=gathered.at[d, :, pl.ds(v0, nv)],
            send_sem=send1.at[c, d], recv_sem=recv1.at[c, d],
            device_id={"inst": to}, device_id_type=MESH,
        )

    def second(c, d):
        v0, nv = CHUNKS[c]
        to = lax.rem(me + d, ND)
        return pltpu.make_async_remote_copy(
            src_ref=turned.at[d, :, pl.ds(v0, nv)],
            dst_ref=spectral.at[:, pl.ds(v0, nv), my_rows],
            send_sem=send2.at[c, d], recv_sem=recv2.at[c, d],
            device_id={"inst": to}, device_id_type=MESH,
        )

    def face_to(r):
        return pltpu.make_async_remote_copy(
            src_ref=payload, dst_ref=faces.at[rank],
            send_sem=face_send.at[r], recv_sem=face_recv.at[rank],
            device_id=across(r), device_id_type=MESH,
        )

    def face_from(r):
        return pltpu.make_async_remote_copy(
            src_ref=payload, dst_ref=faces.at[r],
            send_sem=face_send.at[r], recv_sem=face_recv.at[r],
            device_id=across(r), device_id_type=MESH,
        )

    def halo_to(i):
        return pltpu.make_async_remote_copy(
            src_ref=edges.at[i], dst_ref=halos.at[i],
            send_sem=halo_send.at[i], recv_sem=halo_recv.at[i],
            device_id=(next_id, prev_id)[i], device_id_type=MESH,
        )

    chunks = range(len(CHUNKS))
    for c in chunks:
        for d in ORDER:
            first(c, d).start()
    for copy in loads:
        copy.wait()

    wide = lax.broadcasted_iota(jnp.int32, (ROWS, LANES), 1)
    outward = coef[3]
    columns = jnp.zeros((ROWS, LANES), jnp.float32)
    for k in range(2 * NV):
        n, u = divmod(k, NV)
        columns = jnp.where(wide == k, pltpu.roll(outward * adj[n, u], k + 1, 1), columns)
        edges[0, k : k + 1, :] = coef[1, ROWS - 1 : ROWS, :] * adj[n, u, ROWS - 1 : ROWS, :]
        edges[1, k : k + 1, :] = coef[2, 0:1, :] * adj[n, u, 0:1, :]
    payload[...] = columns.T[0:16, :]
    for i in range(2):
        edges[i, 2 * NV : 16, :] = jnp.zeros((16 - 2 * NV, LANES), jnp.float32)

    def send_across(r, carry):
        face_to(r).start()
        return carry

    lax.fori_loop(0, earlier, send_across, 0)
    pl.when(next_earlier)(lambda: halo_to(0).start())
    pl.when(prev_earlier)(lambda: halo_to(1).start())

    lane = lax.broadcasted_iota(jnp.int32, (BLK, LANES), 1)

    def stencil(step, carry):
        n = step // (ROWS // BLK)
        rows = pl.ds(pl.multiple_of(lax.rem(step, ROWS // BLK) * BLK, BLK), BLK)
        field = [adj[n, u, rows, :] for u in range(NV)]
        total = [base[n, v, rows, :] for v in range(NV)]
        for k in range(5):
            scale = coef[k, rows, :]
            q = [scale * f for f in field]
            for v in range(NV):
                mixed = mixing[k, 0, v] * q[0]
                for u in range(1, NV):
                    mixed = mixed + mixing[k, u, v] * q[u]
                if k == 0:
                    total[v] = total[v] + mixed
                elif k == 1:
                    ahead[n, v, rows, :] = mixed
                elif k == 2:
                    behind[n, v, rows, :] = mixed
                elif k == 3:
                    total[v] = total[v] + jnp.where(lane == 0, 0.0, pltpu.roll(mixed, 1, 1))
                else:
                    total[v] = total[v] + jnp.where(lane == LANES - 1, 0.0, pltpu.roll(mixed, LANES - 1, 1))
        for v in range(NV):
            base[n, v, rows, :] = total[v]
        return carry

    lax.fori_loop(0, 2 * (ROWS // BLK), stencil, 0)

    row = lax.broadcasted_iota(jnp.int32, (ROWS, LANES), 0)

    def moved(step, carry):
        n, v = step // NV, lax.rem(step, NV)
        down = jnp.where(row == 0, 0.0, pltpu.roll(ahead[n, v], 1, 0))
        up = jnp.where(row == ROWS - 1, 0.0, pltpu.roll(behind[n, v], ROWS - 1, 0))
        base[n, v] = base[n, v] + (down + up)
        return carry

    lax.fori_loop(0, 2 * NV, moved, 0)

    entries = spectral_entries()
    half = NI // 2

    def transform(c):
        v0, nv = CHUNKS[c]

        def body(step, carry):
            v = v0 + step // 2
            part = lax.rem(step, 2) * 8
            rows = pl.ds(pl.multiple_of(part, 8), 8)
            mine = pl.ds(pl.multiple_of(me * BLK + part, 8), 8)
            x = []
            for a in range(NI):
                slot, i = (-(a // 2)) % ND, a % 2
                x.append(adj[i, v, mine, :] if slot == 0 else gathered[slot, i, v, rows, :])
            plus = [x[a] + x[a + half] for a in range(half)]
            minus = [x[a] - x[a + half] for a in range(half)]
            for b in range(half):
                even, odd = None, None
                for a in range(half):
                    low, high = entries[(a - b) % NI], entries[(a + half - b) % NI]
                    even_term = np.float32(0.5 * (low + high)) * plus[a]
                    odd_term = np.float32(0.5 * (low - high)) * minus[a]
                    even = even_term if even is None else even + even_term
                    odd = odd_term if odd is None else odd + odd_term
                for n, value in ((b, even + odd), (b + half, even - odd)):
                    slot, j = n // 2, n % 2
                    if slot == 0:
                        spectral[j, v, mine, :] = value
                    else:
                        turned[slot, j, v, rows, :] = value
            return carry

        lax.fori_loop(0, 2 * nv, body, 0)

    for c in chunks:
        for d in ORDER:
            first(c, d).wait_recv()
        transform(c)
        for d in ORDER:
            second(c, d).start()

    def answer_across(r, carry):
        face_from(r).wait_recv()
        face_to(r).start()
        return carry

    def answer_next():
        halo_to(1).wait_recv()
        halo_to(0).start()

    def answer_prev():
        halo_to(0).wait_recv()
        halo_to(1).start()

    pl.when(jnp.logical_not(next_earlier))(answer_next)
    pl.when(jnp.logical_not(prev_earlier))(answer_prev)
    lax.fori_loop(earlier, SECTORS, answer_across, 0)

    def take_across(r, carry):
        face_from(r).wait_recv()
        return carry

    pl.when(next_earlier)(lambda: halo_to(1).wait_recv())
    pl.when(prev_earlier)(lambda: halo_to(0).wait_recv())
    lax.fori_loop(0, earlier, take_across, 0)

    thin = lax.broadcasted_iota(jnp.int32, (16, LANES), 1) // FB
    mixed = []
    for n in range(2):
        rows = jnp.zeros((16, LANES), jnp.float32)
        for b in range(NB):
            block = partner[n, NB * p + b]
            sector, kind = block // (2 * NB), lax.rem(block, NB)
            face = faces[lax.rem(sector, NZ) * NX + sector // NZ]
            for turn in range(NB):
                here = jnp.logical_and(thin == b, kind == (b - turn) % NB)
                rows = jnp.where(here, pltpu.roll(face, turn * FB, 1) if turn else face, rows)
        for v in range(NV):
            mixed.append(sum(mixing[3, u, v] * rows[n * NV + u : n * NV + u + 1, :] for u in range(NV)))
    mixed = jnp.concatenate(mixed + [jnp.zeros((LANES - 2 * NV, LANES), jnp.float32)], axis=0).T
    for k in range(2 * NV):
        n, v = divmod(k, NV)
        column = pltpu.roll(mixed, LANES - 1 - k, 1)
        base[n, v] = base[n, v] + jnp.where(wide == LANES - 1, column, 0.0)
        first_row = sum(mixing[1, u, v] * halos[0, n * NV + u : n * NV + u + 1, :] for u in range(NV))
        last_row = sum(mixing[2, u, v] * halos[1, n * NV + u : n * NV + u + 1, :] for u in range(NV))
        base[n, v, 0:1, :] = base[n, v, 0:1, :] + first_row
        base[n, v, ROWS - 1 : ROWS, :] = base[n, v, ROWS - 1 : ROWS, :] + last_row

    stores = []
    for c in chunks:
        v0, nv = CHUNKS[c]
        for d in ORDER:
            second(c, d).wait_recv()

        def finish(step, carry, v0=v0):
            v = v0 + step // 2
            n = lax.rem(step, 2)
            base[n, v] = base[n, v] + (SPIN_RATE * vol[...]) * spectral[n, v]
            return carry

        lax.fori_loop(0, 2 * nv, finish, 0)
        store = pltpu.make_async_copy(
            base.at[:, pl.ds(v0, nv)], out_hbm.at[:, pl.ds(v0, nv)], store_sem.at[c]
        )
        store.start()
        stores.append(store)
    for c in chunks:
        for d in ORDER:
            first(c, d).wait_send()
            second(c, d).wait_send()

    def sent_across(r, carry):
        face_to(r).wait_send()
        return carry

    lax.fori_loop(0, SECTORS, sent_across, 0)
    for i in range(2):
        halo_to(i).wait_send()
    for store in stores:
        store.wait()


def local(adjoint, source, coefficient, volume, mixing, face_partner):
    f32 = jnp.float32
    hbm = pl.BlockSpec(memory_space=pltpu.HBM)
    shard = (2, NV, ROWS, LANES)
    nc = len(CHUNKS)
    given = (adjoint, source, coefficient, volume, mixing, face_partner)
    operands = [pltpu.with_memory_space_constraint(t, pltpu.HBM) for t in given]
    return pl.pallas_call(
        main_kernel,
        out_shape=jax.ShapeDtypeStruct(shard, f32),
        in_specs=[hbm] * 6,
        out_specs=hbm,
        scratch_shapes=[
            pltpu.VMEM(shard, f32), pltpu.VMEM(shard, f32),
            pltpu.VMEM((5, ROWS, LANES), f32), pltpu.VMEM((ROWS, LANES), f32),
            pltpu.VMEM(shard, f32), pltpu.VMEM(shard, f32),
            pltpu.VMEM((ND, 2, NV, BLK, LANES), f32), pltpu.VMEM((ND, 2, NV, BLK, LANES), f32),
            pltpu.VMEM(shard, f32),
            pltpu.VMEM((16, LANES), f32), pltpu.VMEM((SECTORS, 16, LANES), f32),
            pltpu.VMEM((2, 16, LANES), f32), pltpu.VMEM((2, 16, LANES), f32),
            pltpu.SMEM((5, NV, NV), f32), pltpu.SMEM((2, SECTORS * 2 * NB), jnp.int32),
            pltpu.SemaphoreType.DMA((6,)), pltpu.SemaphoreType.DMA((nc,)),
            pltpu.SemaphoreType.DMA((nc, ND)), pltpu.SemaphoreType.DMA((nc, ND)),
            pltpu.SemaphoreType.DMA((nc, ND)), pltpu.SemaphoreType.DMA((nc, ND)),
            pltpu.SemaphoreType.DMA((SECTORS,)), pltpu.SemaphoreType.DMA((SECTORS,)),
            pltpu.SemaphoreType.DMA((2,)), pltpu.SemaphoreType.DMA((2,)),
        ],
        compiler_params=pltpu.CompilerParams(
            collective_id=0, has_side_effects=True, vmem_limit_bytes=VMEM_LIMIT
        ),
        cost_estimate=pl.CostEstimate(flops=20_000_000, bytes_accessed=60_000_000, transcendentals=0),
        name="residual",
    )(*operands)


def solution(mesh):
    in_specs = (
        P("inst", None, "space", None),
        P("inst", None, "space", None),
        P(None, "space", None),
        P("space", None),
        P(),
        P("inst", None),
    )
    out_specs = P("inst", None, "space", None)
    return jax.shard_map(local, mesh=mesh, in_specs=in_specs, out_specs=out_specs, check_vma=False)
```

```python
import functools

import numpy as np

import jax
import jax.numpy as jnp
from jax import lax
from jax.experimental import pallas as pl
from jax.experimental.pallas import tpu as pltpu
from jax.sharding import PartitionSpec as P

MESH = pl.DeviceIdType.MESH
NI = 16
ND = 8
NX = 4
NZ = 8
SECTORS = NX * NZ
SPACE = 2 * SECTORS
NV = 5
NB = 4
FB = 32
BLK = 16
ROWS = 128
LANES = 128
SPIN_RATE = 0.75
CHUNKS = ((0, 3), (3, 2))
ORDER = (4, 3, 5, 2, 6, 1, 7)
VMEM_LIMIT = 16 * 1024 * 1024


def spectral_entries():
    offset = np.arange(1, NI)
    angle = np.pi * offset / NI
    entries = 0.5 * np.where(offset % 2 == 0, 1.0, -1.0) * np.cos(angle) / np.sin(angle)
    return np.concatenate([[0.0], entries])


def main_kernel(
    adj_hbm, src_hbm, coef_hbm, vol_hbm, mixing_hbm, partner_hbm, out_hbm,
    adj, base, coef, vol, ahead, behind, gathered, turned, spectral, payload, faces, edges, halos,
    mixing, partner,
    load_sem, store_sem, send1, recv1, send2, recv2, face_send, face_recv, halo_send, halo_recv, heard, column_in, columns_in, all_in,
):
    me = lax.axis_index("inst")
    p = lax.axis_index("space")
    side = lax.rem(p, 2)
    z, x = lax.rem(p // 2, NZ), p // (2 * NZ)
    sector = x * NZ + z
    is_hub = z == 0
    is_chief = jnp.logical_and(is_hub, jnp.logical_and(x == 0, side == 1))
    next_earlier, prev_earlier = z == NZ - 1, z != 0
    next_id = {"space": lax.rem(p + 2, SPACE)}
    prev_id = {"space": lax.rem(p + SPACE - 2, SPACE)}

    def at(x, z, side):
        return {"space": 2 * (x * NZ + z) + side}

    def over_hubs(act):
        for other in range(NX):
            if other:
                act(at(other, 0, 1))
            act(at(other, 0, 0))

    def over_column(act):
        for other in range(1, NZ):
            act(at(x, other, side))

    barrier = pltpu.get_barrier_semaphore()

    def greet(device):
        pl.semaphore_signal(barrier, inc=1, device_id=device, device_id_type=MESH)

    up, down = {"inst": lax.rem(me + 1, ND)}, {"inst": lax.rem(me + ND - 1, ND)}
    greet(up)
    greet(down)

    pl.when(is_chief)(lambda: over_hubs(greet))
    pl.when(is_hub)(lambda: over_column(greet))
    pl.when(jnp.logical_not(next_earlier))(lambda: greet(next_id))
    pl.when(jnp.logical_not(prev_earlier))(lambda: greet(prev_id))
    loads = [
        pltpu.make_async_copy(s, t, load_sem.at[i])
        for i, (s, t) in enumerate((
            (adj_hbm, adj), (coef_hbm, coef), (src_hbm, base), (vol_hbm, vol),
            (mixing_hbm, mixing), (partner_hbm, partner),
        ))
    ]
    for copy in loads:
        copy.start()
    greetings = jnp.where(is_hub, 1 - is_chief.astype(jnp.int32), 2 + next_earlier.astype(jnp.int32))
    pl.semaphore_wait(barrier, 2 + greetings)

    my_rows = pl.ds(pl.multiple_of(me * BLK, BLK), BLK)

    def first(c, d):
        v0, nv = CHUNKS[c]
        to = lax.rem(me + d, ND)
        return pltpu.make_async_remote_copy(
            src_ref=adj_hbm.at[:, pl.ds(v0, nv), pl.ds(pl.multiple_of(to * BLK, BLK), BLK)],
            dst_ref=gathered.at[d, :, pl.ds(v0, nv)],
            send_sem=send1.at[c, d], recv_sem=recv1.at[c, d],
            device_id={"inst": to}, device_id_type=MESH,
        )

    def second(c, d):
        v0, nv = CHUNKS[c]
        to = lax.rem(me + d, ND)
        return pltpu.make_async_remote_copy(
            src_ref=turned.at[d, :, pl.ds(v0, nv)],
            dst_ref=spectral.at[:, pl.ds(v0, nv), my_rows],
            send_sem=send2.at[c, d], recv_sem=recv2.at[c, d],
            device_id={"inst": to}, device_id_type=MESH,
        )

    def face_to(other):
        return pltpu.make_async_remote_copy(
            src_ref=payload, dst_ref=faces.at[sector],
            send_sem=face_send.at[other], recv_sem=face_recv.at[sector],
            device_id={"space": 2 * other + 1 - side}, device_id_type=MESH,
        )

    def face_from(other):
        return pltpu.make_async_remote_copy(
            src_ref=payload, dst_ref=faces.at[other],
            send_sem=face_send.at[other], recv_sem=face_recv.at[other],
            device_id={"space": 2 * other + 1 - side}, device_id_type=MESH,
        )

    def halo_to(i):
        return pltpu.make_async_remote_copy(
            src_ref=edges.at[i], dst_ref=halos.at[i],
            send_sem=halo_send.at[i], recv_sem=halo_recv.at[i],
            device_id=(next_id, prev_id)[i], device_id_type=MESH,
        )

    chunks = range(len(CHUNKS))

    def heard_of(i):
        pl.semaphore_wait(heard.at[i], 1)

    def signal(semaphore, device):
        pl.semaphore_signal(semaphore, inc=1, device_id=device, device_id_type=MESH)

    def tell(device, i):
        signal(heard.at[i], device)

    tell(down, 0)
    tell(up, 1)
    first(0, 1).start()
    first(0, ND - 1).start()
    heard_of(0)
    tell(down, 2)
    first(0, 2).start()
    heard_of(1)
    tell(up, 3)
    first(0, ND - 2).start()
    heard_of(2)
    tell(down, 4)
    first(0, 3).start()
    heard_of(3)
    first(0, ND - 3).start()
    heard_of(4)
    first(0, 4).start()
    pl.when(jnp.logical_not(is_hub))(lambda: signal(column_in, at(x, 0, side)))
    for c in chunks[1:]:
        for d in ORDER:
            first(c, d).start()
    for copy in loads:
        copy.wait()

    wide = lax.broadcasted_iota(jnp.int32, (ROWS, LANES), 1)
    outward = coef[3]
    columns = jnp.zeros((ROWS, LANES), jnp.float32)
    for k in range(2 * NV):
        n, u = divmod(k, NV)
        columns = jnp.where(wide == k, pltpu.roll(outward * adj[n, u], k + 1, 1), columns)
        edges[0, k : k + 1, :] = coef[1, ROWS - 1 : ROWS, :] * adj[n, u, ROWS - 1 : ROWS, :]
        edges[1, k : k + 1, :] = coef[2, 0:1, :] * adj[n, u, 0:1, :]
    payload[...] = columns.T[0 : 2 * NV, :]

    pl.when(next_earlier)(lambda: halo_to(0).start())
    pl.when(prev_earlier)(lambda: halo_to(1).start())

    lane = lax.broadcasted_iota(jnp.int32, (BLK, LANES), 1)

    def stencil(step, carry):
        n = step // (ROWS // BLK)
        rows = pl.ds(pl.multiple_of(lax.rem(step, ROWS // BLK) * BLK, BLK), BLK)
        field = [adj[n, u, rows, :] for u in range(NV)]
        total = [base[n, v, rows, :] for v in range(NV)]
        for k in range(5):
            scale = coef[k, rows, :]
            q = [scale * f for f in field]
            for v in range(NV):
                mixed = mixing[k, 0, v] * q[0]
                for u in range(1, NV):
                    mixed = mixed + mixing[k, u, v] * q[u]
                if k == 0:
                    total[v] = total[v] + mixed
                elif k == 1:
                    ahead[n, v, rows, :] = mixed
                elif k == 2:
                    behind[n, v, rows, :] = mixed
                elif k == 3:
                    total[v] = total[v] + jnp.where(lane == 0, 0.0, pltpu.roll(mixed, 1, 1))
                else:
                    total[v] = total[v] + jnp.where(lane == LANES - 1, 0.0, pltpu.roll(mixed, LANES - 1, 1))
        for v in range(NV):
            base[n, v, rows, :] = total[v]
        return carry

    lax.fori_loop(0, 2 * (ROWS // BLK), stencil, 0)

    row = lax.broadcasted_iota(jnp.int32, (ROWS, LANES), 0)

    def moved(step, carry):
        n, v = step // NV, lax.rem(step, NV)
        down = jnp.where(row == 0, 0.0, pltpu.roll(ahead[n, v], 1, 0))
        up = jnp.where(row == ROWS - 1, 0.0, pltpu.roll(behind[n, v], ROWS - 1, 0))
        base[n, v] = base[n, v] + (down + up)
        return carry

    lax.fori_loop(0, 2 * NV, moved, 0)

    def report():
        pl.semaphore_wait(column_in, NZ - 1)
        pl.when(jnp.logical_not(is_chief))(lambda: signal(columns_in, at(0, 0, 1)))

    def spread():
        pl.semaphore_wait(columns_in, 2 * NX - 1)
        over_hubs(lambda device: signal(all_in, device))

    def send_faces():
        pl.when(jnp.logical_not(is_chief))(lambda: pl.semaphore_wait(all_in, 1))
        pl.when(is_hub)(lambda: over_column(lambda device: signal(all_in, device)))

        def send_face(other, carry):
            face_to(other).start()
            return carry

        lax.fori_loop(0, SECTORS, send_face, 0)

    pl.when(is_hub)(report)

    entries = spectral_entries()
    half = NI // 2

    def transform(c):
        v0, nv = CHUNKS[c]

        def body(step, carry):
            v = v0 + step // 2
            part = lax.rem(step, 2) * 8
            rows = pl.ds(pl.multiple_of(part, 8), 8)
            mine = pl.ds(pl.multiple_of(me * BLK + part, 8), 8)
            x = []
            for a in range(NI):
                slot, i = (-(a // 2)) % ND, a % 2
                x.append(adj[i, v, mine, :] if slot == 0 else gathered[slot, i, v, rows, :])
            plus = [x[a] + x[a + half] for a in range(half)]
            minus = [x[a] - x[a + half] for a in range(half)]
            for b in range(half):
                even, odd = None, None
                for a in range(half):
                    low, high = entries[(a - b) % NI], entries[(a + half - b) % NI]
                    even_term = np.float32(0.5 * (low + high)) * plus[a]
                    odd_term = np.float32(0.5 * (low - high)) * minus[a]
                    even = even_term if even is None else even + even_term
                    odd = odd_term if odd is None else odd + odd_term
                for n, value in ((b, even + odd), (b + half, even - odd)):
                    slot, j = n // 2, n % 2
                    if slot == 0:
                        spectral[j, v, mine, :] = value
                    else:
                        turned[slot, j, v, rows, :] = value
            return carry

        lax.fori_loop(0, 2 * nv, body, 0)

    for c in chunks:
        for d in ORDER:
            first(c, d).wait_recv()
        transform(c)
        for d in ORDER:
            second(c, d).start()
        if c == 0:
            pl.when(is_chief)(spread)
            send_faces()

    def answer_next():
        halo_to(1).wait_recv()
        halo_to(0).start()

    def answer_prev():
        halo_to(0).wait_recv()
        halo_to(1).start()

    pl.when(jnp.logical_not(next_earlier))(answer_next)
    pl.when(jnp.logical_not(prev_earlier))(answer_prev)

    pl.when(next_earlier)(lambda: halo_to(1).wait_recv())
    pl.when(prev_earlier)(lambda: halo_to(0).wait_recv())

    def take_face(other, carry):
        face_from(other).wait_recv()
        return carry

    lax.fori_loop(0, SECTORS, take_face, 0)

    thin = lax.broadcasted_iota(jnp.int32, (2 * NV, LANES), 1) // FB
    mixed = []
    for n in range(2):
        rows = jnp.zeros((2 * NV, LANES), jnp.float32)
        for b in range(NB):
            block = partner[n, NB * p + b]
            face, kind = faces[block // (2 * NB)], lax.rem(block, NB)
            for turn in range(NB):
                here = jnp.logical_and(thin == b, kind == (b - turn) % NB)
                rows = jnp.where(here, pltpu.roll(face, turn * FB, 1) if turn else face, rows)
        for v in range(NV):
            mixed.append(sum(mixing[3, u, v] * rows[n * NV + u : n * NV + u + 1, :] for u in range(NV)))
    mixed = jnp.concatenate(mixed + [jnp.zeros((LANES - 2 * NV, LANES), jnp.float32)], axis=0).T
    for k in range(2 * NV):
        n, v = divmod(k, NV)
        column = pltpu.roll(mixed, LANES - 1 - k, 1)
        base[n, v] = base[n, v] + jnp.where(wide == LANES - 1, column, 0.0)
        first_row = sum(mixing[1, u, v] * halos[0, n * NV + u : n * NV + u + 1, :] for u in range(NV))
        last_row = sum(mixing[2, u, v] * halos[1, n * NV + u : n * NV + u + 1, :] for u in range(NV))
        base[n, v, 0:1, :] = base[n, v, 0:1, :] + first_row
        base[n, v, ROWS - 1 : ROWS, :] = base[n, v, ROWS - 1 : ROWS, :] + last_row

    stores = []
    for c in chunks:
        v0, nv = CHUNKS[c]
        for d in ORDER:
            second(c, d).wait_recv()

        def finish(step, carry, v0=v0):
            v = v0 + step // 2
            n = lax.rem(step, 2)
            base[n, v] = base[n, v] + (SPIN_RATE * vol[...]) * spectral[n, v]
            return carry

        lax.fori_loop(0, 2 * nv, finish, 0)
        store = pltpu.make_async_copy(
            base.at[:, pl.ds(v0, nv)], out_hbm.at[:, pl.ds(v0, nv)], store_sem.at[c]
        )
        store.start()
        stores.append(store)
    for c in chunks:
        for d in ORDER:
            first(c, d).wait_send()
            second(c, d).wait_send()

    def sent_face(other, carry):
        face_to(other).wait_send()
        return carry

    lax.fori_loop(0, SECTORS, sent_face, 0)
    for i in range(2):
        halo_to(i).wait_send()
    for store in stores:
        store.wait()


def local(adjoint, source, coefficient, volume, mixing, face_partner):
    f32 = jnp.float32
    hbm = pl.BlockSpec(memory_space=pltpu.HBM)
    shard = (2, NV, ROWS, LANES)
    nc = len(CHUNKS)
    given = (adjoint, source, coefficient, volume, mixing, face_partner)
    operands = [pltpu.with_memory_space_constraint(t, pltpu.HBM) for t in given]
    return pl.pallas_call(
        main_kernel,
        out_shape=jax.ShapeDtypeStruct(shard, f32),
        in_specs=[hbm] * 6,
        out_specs=hbm,
        scratch_shapes=[
            pltpu.VMEM(shard, f32), pltpu.VMEM(shard, f32),
            pltpu.VMEM((5, ROWS, LANES), f32), pltpu.VMEM((ROWS, LANES), f32),
            pltpu.VMEM(shard, f32), pltpu.VMEM(shard, f32),
            pltpu.VMEM((ND, 2, NV, BLK, LANES), f32), pltpu.VMEM((ND, 2, NV, BLK, LANES), f32),
            pltpu.VMEM(shard, f32),
            pltpu.VMEM((2 * NV, LANES), f32), pltpu.VMEM((SECTORS, 2 * NV, LANES), f32),
            pltpu.VMEM((2, 2 * NV, LANES), f32), pltpu.VMEM((2, 2 * NV, LANES), f32),
            pltpu.SMEM((5, NV, NV), f32), pltpu.SMEM((2, SECTORS * 2 * NB), jnp.int32),
            pltpu.SemaphoreType.DMA((6,)), pltpu.SemaphoreType.DMA((nc,)),
            pltpu.SemaphoreType.DMA((nc, ND)), pltpu.SemaphoreType.DMA((nc, ND)),
            pltpu.SemaphoreType.DMA((nc, ND)), pltpu.SemaphoreType.DMA((nc, ND)),
            pltpu.SemaphoreType.DMA((SECTORS,)), pltpu.SemaphoreType.DMA((SECTORS,)),
            pltpu.SemaphoreType.DMA((2,)), pltpu.SemaphoreType.DMA((2,)),
            pltpu.SemaphoreType.REGULAR((5,)),
            pltpu.SemaphoreType.REGULAR, pltpu.SemaphoreType.REGULAR, pltpu.SemaphoreType.REGULAR,
        ],
        compiler_params=pltpu.CompilerParams(
            collective_id=0, has_side_effects=True, vmem_limit_bytes=VMEM_LIMIT
        ),
        cost_estimate=pl.CostEstimate(flops=20_000_000, bytes_accessed=60_000_000, transcendentals=0),
        name="residual",
    )(*operands)


def solution(mesh):
    in_specs = (
        P("inst", None, "space", None),
        P("inst", None, "space", None),
        P(None, "space", None),
        P("space", None),
        P(),
        P("inst", None),
    )
    out_specs = P("inst", None, "space", None)
    return jax.shard_map(local, mesh=mesh, in_specs=in_specs, out_specs=out_specs, check_vma=False)
```

```python
import functools

import numpy as np

import jax
import jax.numpy as jnp
from jax import lax
from jax.experimental import pallas as pl
from jax.experimental.pallas import tpu as pltpu
from jax.sharding import PartitionSpec as P

MESH = pl.DeviceIdType.MESH
NI = 16
ND = 8
NX = 4
NZ = 8
SECTORS = NX * NZ
SPACE = 2 * SECTORS
NV = 5
NB = 4
FB = 32
BLK = 16
ROWS = 128
LANES = 128
SPIN_RATE = 0.75
KNOWN = {4: (0, 1, 2), 5: (0, 1), 6: (0, 1), 7: (1,), 3: (0,)}
CHUNKS = ((0, 3), (3, 2))
ORDER = (4, 3, 5, 2, 6, 1, 7)
VMEM_LIMIT = 16 * 1024 * 1024


def spectral_entries():
    offset = np.arange(1, NI)
    angle = np.pi * offset / NI
    entries = 0.5 * np.where(offset % 2 == 0, 1.0, -1.0) * np.cos(angle) / np.sin(angle)
    return np.concatenate([[0.0], entries])


def main_kernel(
    adj_hbm, src_hbm, coef_hbm, vol_hbm, mixing_hbm, partner_hbm, out_hbm,
    adj, base, coef, vol, ahead, behind, gathered, turned, spectral, payload, faces, edges, halos,
    mixing, partner,
    load_sem, store_sem, send1, recv1, send2, recv2, face_send, face_recv, halo_send, halo_recv, heard, column_in, columns_in, all_in,
):
    me = lax.axis_index("inst")
    p = lax.axis_index("space")
    side = lax.rem(p, 2)
    z, x = lax.rem(p // 2, NZ), p // (2 * NZ)
    sector = x * NZ + z
    is_hub = z == 0
    is_chief = jnp.logical_and(is_hub, jnp.logical_and(x == 0, side == 1))
    next_earlier, prev_earlier = z == NZ - 1, z != 0
    next_id = {"space": lax.rem(p + 2, SPACE)}
    prev_id = {"space": lax.rem(p + SPACE - 2, SPACE)}

    def at(x, z, side):
        return {"space": 2 * (x * NZ + z) + side}

    def over_hubs(act):
        for other in range(NX):
            if other:
                act(at(other, 0, 1))
            act(at(other, 0, 0))

    def over_column(act):
        for other in range(1, NZ):
            act(at(x, other, side))

    barrier = pltpu.get_barrier_semaphore()

    def greet(device):
        pl.semaphore_signal(barrier, inc=1, device_id=device, device_id_type=MESH)

    up, down = {"inst": lax.rem(me + 1, ND)}, {"inst": lax.rem(me + ND - 1, ND)}
    greet(up)
    greet(down)
    for early in range(ND):
        later = [late for late in KNOWN if early in KNOWN[late]]
        if later:

            @pl.when(me == early)
            def greet_later(later=later):
                for late in later:
                    greet({"inst": late})


    pl.when(is_chief)(lambda: over_hubs(greet))
    pl.when(is_hub)(lambda: over_column(greet))
    pl.when(jnp.logical_not(next_earlier))(lambda: greet(next_id))
    pl.when(jnp.logical_not(prev_earlier))(lambda: greet(prev_id))
    loads = [
        pltpu.make_async_copy(s, t, load_sem.at[i])
        for i, (s, t) in enumerate((
            (adj_hbm, adj), (coef_hbm, coef), (src_hbm, base), (vol_hbm, vol),
            (mixing_hbm, mixing), (partner_hbm, partner),
        ))
    ]
    for copy in loads:
        copy.start()
    greetings = jnp.where(is_hub, 1 - is_chief.astype(jnp.int32), 2 + next_earlier.astype(jnp.int32))
    for late in KNOWN:
        greetings = greetings + jnp.where(me == late, len(KNOWN[late]), 0)
    pl.semaphore_wait(barrier, 2 + greetings)

    my_rows = pl.ds(pl.multiple_of(me * BLK, BLK), BLK)

    def first(c, d):
        v0, nv = CHUNKS[c]
        to = lax.rem(me + d, ND)
        return pltpu.make_async_remote_copy(
            src_ref=adj_hbm.at[:, pl.ds(v0, nv), pl.ds(pl.multiple_of(to * BLK, BLK), BLK)],
            dst_ref=gathered.at[d, :, pl.ds(v0, nv)],
            send_sem=send1.at[c, d], recv_sem=recv1.at[c, d],
            device_id={"inst": to}, device_id_type=MESH,
        )

    def second(c, d):
        v0, nv = CHUNKS[c]
        to = lax.rem(me + d, ND)
        return pltpu.make_async_remote_copy(
            src_ref=turned.at[d, :, pl.ds(v0, nv)],
            dst_ref=spectral.at[:, pl.ds(v0, nv), my_rows],
            send_sem=send2.at[c, d], recv_sem=recv2.at[c, d],
            device_id={"inst": to}, device_id_type=MESH,
        )

    def face_to(other):
        return pltpu.make_async_remote_copy(
            src_ref=payload, dst_ref=faces.at[sector],
            send_sem=face_send.at[other], recv_sem=face_recv.at[sector],
            device_id={"space": 2 * other + 1 - side}, device_id_type=MESH,
        )

    def face_from(other):
        return pltpu.make_async_remote_copy(
            src_ref=payload, dst_ref=faces.at[other],
            send_sem=face_send.at[other], recv_sem=face_recv.at[other],
            device_id={"space": 2 * other + 1 - side}, device_id_type=MESH,
        )

    def halo_to(i):
        return pltpu.make_async_remote_copy(
            src_ref=edges.at[i], dst_ref=halos.at[i],
            send_sem=halo_send.at[i], recv_sem=halo_recv.at[i],
            device_id=(next_id, prev_id)[i], device_id_type=MESH,
        )

    chunks = range(len(CHUNKS))

    def heard_of(i):
        pl.semaphore_wait(heard.at[i], 1)

    def signal(semaphore, device):
        pl.semaphore_signal(semaphore, inc=1, device_id=device, device_id_type=MESH)

    def tell(device, i):
        signal(heard.at[i], device)

    def unless_known(d):
        known = me == -1
        for late in KNOWN:
            if (late + d) % ND in KNOWN[late]:
                known = jnp.logical_or(known, me == late)
        pl.when(jnp.logical_not(known))(lambda: first(0, d).start())

    tell(down, 0)
    tell(up, 1)
    first(0, 1).start()
    first(0, ND - 1).start()
    for late in KNOWN:

        @pl.when(me == late)
        def send_known(late=late):
            for early in KNOWN[late]:
                first(0, (early - late) % ND).start()

    heard_of(0)
    tell(down, 2)
    unless_known(2)
    heard_of(1)
    tell(up, 3)
    unless_known(ND - 2)
    heard_of(2)
    tell(down, 4)
    unless_known(3)
    heard_of(3)
    unless_known(ND - 3)
    heard_of(4)
    unless_known(4)
    pl.when(jnp.logical_not(is_hub))(lambda: signal(column_in, at(x, 0, side)))
    for c in chunks[1:]:
        for d in ORDER:
            first(c, d).start()
    for copy in loads:
        copy.wait()

    wide = lax.broadcasted_iota(jnp.int32, (ROWS, LANES), 1)
    outward = coef[3]
    columns = jnp.zeros((ROWS, LANES), jnp.float32)
    for k in range(2 * NV):
        n, u = divmod(k, NV)
        columns = jnp.where(wide == k, pltpu.roll(outward * adj[n, u], k + 1, 1), columns)
        edges[0, k : k + 1, :] = coef[1, ROWS - 1 : ROWS, :] * adj[n, u, ROWS - 1 : ROWS, :]
        edges[1, k : k + 1, :] = coef[2, 0:1, :] * adj[n, u, 0:1, :]
    payload[...] = columns.T[0 : 2 * NV, :]

    pl.when(next_earlier)(lambda: halo_to(0).start())
    pl.when(prev_earlier)(lambda: halo_to(1).start())

    lane = lax.broadcasted_iota(jnp.int32, (BLK, LANES), 1)

    def stencil(step, carry):
        n = step // (ROWS // BLK)
        rows = pl.ds(pl.multiple_of(lax.rem(step, ROWS // BLK) * BLK, BLK), BLK)
        field = [adj[n, u, rows, :] for u in range(NV)]
        total = [base[n, v, rows, :] for v in range(NV)]
        for k in range(5):
            scale = coef[k, rows, :]
            q = [scale * f for f in field]
            for v in range(NV):
                mixed = mixing[k, 0, v] * q[0]
                for u in range(1, NV):
                    mixed = mixed + mixing[k, u, v] * q[u]
                if k == 0:
                    total[v] = total[v] + mixed
                elif k == 1:
                    ahead[n, v, rows, :] = mixed
                elif k == 2:
                    behind[n, v, rows, :] = mixed
                elif k == 3:
                    total[v] = total[v] + jnp.where(lane == 0, 0.0, pltpu.roll(mixed, 1, 1))
                else:
                    total[v] = total[v] + jnp.where(lane == LANES - 1, 0.0, pltpu.roll(mixed, LANES - 1, 1))
        for v in range(NV):
            base[n, v, rows, :] = total[v]
        return carry

    lax.fori_loop(0, 2 * (ROWS // BLK), stencil, 0)

    row = lax.broadcasted_iota(jnp.int32, (ROWS, LANES), 0)

    def moved(step, carry):
        n, v = step // NV, lax.rem(step, NV)
        down = jnp.where(row == 0, 0.0, pltpu.roll(ahead[n, v], 1, 0))
        up = jnp.where(row == ROWS - 1, 0.0, pltpu.roll(behind[n, v], ROWS - 1, 0))
        base[n, v] = base[n, v] + (down + up)
        return carry

    lax.fori_loop(0, 2 * NV, moved, 0)

    def report():
        pl.semaphore_wait(column_in, NZ - 1)
        pl.when(jnp.logical_not(is_chief))(lambda: signal(columns_in, at(0, 0, 1)))

    def spread():
        pl.semaphore_wait(columns_in, 2 * NX - 1)
        over_hubs(lambda device: signal(all_in, device))

    def send_faces():
        pl.when(jnp.logical_not(is_chief))(lambda: pl.semaphore_wait(all_in, 1))
        pl.when(is_hub)(lambda: over_column(lambda device: signal(all_in, device)))

        def send_face(other, carry):
            face_to(other).start()
            return carry

        lax.fori_loop(0, SECTORS, send_face, 0)

    pl.when(is_hub)(report)

    entries = spectral_entries()
    half = NI // 2

    def transform(c):
        v0, nv = CHUNKS[c]

        def body(step, carry):
            v = v0 + step // 2
            part = lax.rem(step, 2) * 8
            rows = pl.ds(pl.multiple_of(part, 8), 8)
            mine = pl.ds(pl.multiple_of(me * BLK + part, 8), 8)
            x = []
            for a in range(NI):
                slot, i = (-(a // 2)) % ND, a % 2
                x.append(adj[i, v, mine, :] if slot == 0 else gathered[slot, i, v, rows, :])
            plus = [x[a] + x[a + half] for a in range(half)]
            minus = [x[a] - x[a + half] for a in range(half)]
            for b in range(half):
                even, odd = None, None
                for a in range(half):
                    low, high = entries[(a - b) % NI], entries[(a + half - b) % NI]
                    even_term = np.float32(0.5 * (low + high)) * plus[a]
                    odd_term = np.float32(0.5 * (low - high)) * minus[a]
                    even = even_term if even is None else even + even_term
                    odd = odd_term if odd is None else odd + odd_term
                for n, value in ((b, even + odd), (b + half, even - odd)):
                    slot, j = n // 2, n % 2
                    if slot == 0:
                        spectral[j, v, mine, :] = value
                    else:
                        turned[slot, j, v, rows, :] = value
            return carry

        lax.fori_loop(0, 2 * nv, body, 0)

    for c in chunks:
        for d in ORDER:
            first(c, d).wait_recv()
        transform(c)
        to_first = lax.rem(ND - me, ND)
        if c:
            pl.when(to_first != 0)(lambda: second(c, to_first).start())
        for core, order in enumerate(((4, 5, 3, 6, 2, 7, 1), (7, 1, 6, 2, 5, 3, 4))):

            @pl.when(side == core)
            def send_back(c=c, order=order):
                for d in order:
                    if c:
                        pl.when(to_first != d)(lambda d=d: second(c, d).start())
                    else:
                        second(c, d).start()

        if c == 0:
            pl.when(is_chief)(spread)
            send_faces()

    def answer_next():
        halo_to(1).wait_recv()
        halo_to(0).start()

    def answer_prev():
        halo_to(0).wait_recv()
        halo_to(1).start()

    pl.when(jnp.logical_not(next_earlier))(answer_next)
    pl.when(jnp.logical_not(prev_earlier))(answer_prev)

    pl.when(next_earlier)(lambda: halo_to(1).wait_recv())
    pl.when(prev_earlier)(lambda: halo_to(0).wait_recv())

    def take_face(other, carry):
        face_from(other).wait_recv()
        return carry

    lax.fori_loop(0, SECTORS, take_face, 0)

    thin = lax.broadcasted_iota(jnp.int32, (2 * NV, LANES), 1) // FB
    mixed = []
    for n in range(2):
        rows = jnp.zeros((2 * NV, LANES), jnp.float32)
        for b in range(NB):
            block = partner[n, NB * p + b]
            face, kind = faces[block // (2 * NB)], lax.rem(block, NB)
            for turn in range(NB):
                here = jnp.logical_and(thin == b, kind == (b - turn) % NB)
                rows = jnp.where(here, pltpu.roll(face, turn * FB, 1) if turn else face, rows)
        for v in range(NV):
            mixed.append(sum(mixing[3, u, v] * rows[n * NV + u : n * NV + u + 1, :] for u in range(NV)))
    mixed = jnp.concatenate(mixed + [jnp.zeros((LANES - 2 * NV, LANES), jnp.float32)], axis=0).T
    for k in range(2 * NV):
        n, v = divmod(k, NV)
        column = pltpu.roll(mixed, LANES - 1 - k, 1)
        base[n, v] = base[n, v] + jnp.where(wide == LANES - 1, column, 0.0)
        first_row = sum(mixing[1, u, v] * halos[0, n * NV + u : n * NV + u + 1, :] for u in range(NV))
        last_row = sum(mixing[2, u, v] * halos[1, n * NV + u : n * NV + u + 1, :] for u in range(NV))
        base[n, v, 0:1, :] = base[n, v, 0:1, :] + first_row
        base[n, v, ROWS - 1 : ROWS, :] = base[n, v, ROWS - 1 : ROWS, :] + last_row

    stores = []
    for c in chunks:
        v0, nv = CHUNKS[c]
        for d in ORDER:
            second(c, d).wait_recv()

        def finish(step, carry, v0=v0):
            v = v0 + step // 2
            n = lax.rem(step, 2)
            base[n, v] = base[n, v] + (SPIN_RATE * vol[...]) * spectral[n, v]
            return carry

        lax.fori_loop(0, 2 * nv, finish, 0)
        store = pltpu.make_async_copy(
            base.at[:, pl.ds(v0, nv)], out_hbm.at[:, pl.ds(v0, nv)], store_sem.at[c]
        )
        store.start()
        stores.append(store)
    for c in chunks:
        for d in ORDER:
            first(c, d).wait_send()
            second(c, d).wait_send()

    def sent_face(other, carry):
        face_to(other).wait_send()
        return carry

    lax.fori_loop(0, SECTORS, sent_face, 0)
    for i in range(2):
        halo_to(i).wait_send()
    for store in stores:
        store.wait()


def local(adjoint, source, coefficient, volume, mixing, face_partner):
    f32 = jnp.float32
    hbm = pl.BlockSpec(memory_space=pltpu.HBM)
    shard = (2, NV, ROWS, LANES)
    nc = len(CHUNKS)
    given = (adjoint, source, coefficient, volume, mixing, face_partner)
    operands = [pltpu.with_memory_space_constraint(t, pltpu.HBM) for t in given]
    return pl.pallas_call(
        main_kernel,
        out_shape=jax.ShapeDtypeStruct(shard, f32),
        in_specs=[hbm] * 6,
        out_specs=hbm,
        scratch_shapes=[
            pltpu.VMEM(shard, f32), pltpu.VMEM(shard, f32),
            pltpu.VMEM((5, ROWS, LANES), f32), pltpu.VMEM((ROWS, LANES), f32),
            pltpu.VMEM(shard, f32), pltpu.VMEM(shard, f32),
            pltpu.VMEM((ND, 2, NV, BLK, LANES), f32), pltpu.VMEM((ND, 2, NV, BLK, LANES), f32),
            pltpu.VMEM(shard, f32),
            pltpu.VMEM((2 * NV, LANES), f32), pltpu.VMEM((SECTORS, 2 * NV, LANES), f32),
            pltpu.VMEM((2, 2 * NV, LANES), f32), pltpu.VMEM((2, 2 * NV, LANES), f32),
            pltpu.SMEM((5, NV, NV), f32), pltpu.SMEM((2, SECTORS * 2 * NB), jnp.int32),
            pltpu.SemaphoreType.DMA((6,)), pltpu.SemaphoreType.DMA((nc,)),
            pltpu.SemaphoreType.DMA((nc, ND)), pltpu.SemaphoreType.DMA((nc, ND)),
            pltpu.SemaphoreType.DMA((nc, ND)), pltpu.SemaphoreType.DMA((nc, ND)),
            pltpu.SemaphoreType.DMA((SECTORS,)), pltpu.SemaphoreType.DMA((SECTORS,)),
            pltpu.SemaphoreType.DMA((2,)), pltpu.SemaphoreType.DMA((2,)),
            pltpu.SemaphoreType.REGULAR((5,)),
            pltpu.SemaphoreType.REGULAR, pltpu.SemaphoreType.REGULAR, pltpu.SemaphoreType.REGULAR,
        ],
        compiler_params=pltpu.CompilerParams(
            collective_id=0, has_side_effects=True, vmem_limit_bytes=VMEM_LIMIT
        ),
        cost_estimate=pl.CostEstimate(flops=20_000_000, bytes_accessed=60_000_000, transcendentals=0),
        name="residual",
    )(*operands)


def solution(mesh):
    in_specs = (
        P("inst", None, "space", None),
        P("inst", None, "space", None),
        P(None, "space", None),
        P("space", None),
        P(),
        P("inst", None),
    )
    out_specs = P("inst", None, "space", None)
    return jax.shard_map(local, mesh=mesh, in_specs=in_specs, out_specs=out_specs, check_vma=False)
```

```python
import functools

import numpy as np

import jax
import jax.numpy as jnp
from jax import lax
from jax.experimental import pallas as pl
from jax.experimental.pallas import tpu as pltpu
from jax.sharding import PartitionSpec as P

MESH = pl.DeviceIdType.MESH
NI = 16
ND = 8
NX = 4
NZ = 8
SECTORS = NX * NZ
SPACE = 2 * SECTORS
NV = 5
NB = 4
FB = 32
BLK = 16
ROWS = 128
LANES = 128
SPIN_RATE = 0.75
KNOWN = {4: (0, 1, 2), 5: (0, 1), 6: (0, 1), 7: (1,), 3: (0,)}
CHUNKS = ((0, 3), (3, 2))
ORDER = (4, 3, 5, 2, 6, 1, 7)
VMEM_LIMIT = 16 * 1024 * 1024


def spectral_entries():
    offset = np.arange(1, NI)
    angle = np.pi * offset / NI
    entries = 0.5 * np.where(offset % 2 == 0, 1.0, -1.0) * np.cos(angle) / np.sin(angle)
    return np.concatenate([[0.0], entries])


def main_kernel(
    adj_hbm, src_hbm, coef_hbm, vol_hbm, mixing_hbm, partner_hbm, out,
    adj, base, coef, vol, ahead, behind, gathered, turned, spectral, payload, faces, edges, halos,
    mixing, partner,
    load_sem, send1, recv1, send2, recv2, face_send, face_recv, halo_send, halo_recv, heard, column_in, columns_in, all_in,
):
    me = lax.axis_index("inst")
    p = lax.axis_index("space")
    side = lax.rem(p, 2)
    z, x = lax.rem(p // 2, NZ), p // (2 * NZ)
    sector = x * NZ + z
    is_hub = z == 0
    is_chief = jnp.logical_and(is_hub, jnp.logical_and(x == 0, side == 1))
    next_earlier, prev_earlier = z == NZ - 1, z != 0
    next_id = {"space": lax.rem(p + 2, SPACE)}
    prev_id = {"space": lax.rem(p + SPACE - 2, SPACE)}

    def at(x, z, side):
        return {"space": 2 * (x * NZ + z) + side}

    def over_hubs(act):
        for other in range(NX):
            if other:
                act(at(other, 0, 1))
            act(at(other, 0, 0))

    def over_column(act):
        for other in range(1, NZ):
            act(at(x, other, side))

    barrier = pltpu.get_barrier_semaphore()

    def greet(device):
        pl.semaphore_signal(barrier, inc=1, device_id=device, device_id_type=MESH)

    up, down = {"inst": lax.rem(me + 1, ND)}, {"inst": lax.rem(me + ND - 1, ND)}
    greet(up)
    greet(down)
    for early in range(ND):
        later = [late for late in KNOWN if early in KNOWN[late]]
        if later:

            @pl.when(me == early)
            def greet_later(later=later):
                for late in later:
                    greet({"inst": late})


    pl.when(is_chief)(lambda: over_hubs(greet))
    pl.when(is_hub)(lambda: over_column(greet))
    pl.when(jnp.logical_not(next_earlier))(lambda: greet(next_id))
    pl.when(jnp.logical_not(prev_earlier))(lambda: greet(prev_id))
    loads = [
        pltpu.make_async_copy(s, t, load_sem.at[i])
        for i, (s, t) in enumerate((
            (adj_hbm, adj), (coef_hbm, coef), (src_hbm, base), (vol_hbm, vol),
            (mixing_hbm, mixing), (partner_hbm, partner),
        ))
    ]
    for copy in loads:
        copy.start()
    greetings = jnp.where(is_hub, 1 - is_chief.astype(jnp.int32), 2 + next_earlier.astype(jnp.int32))
    for late in KNOWN:
        greetings = greetings + jnp.where(me == late, len(KNOWN[late]), 0)
    pl.semaphore_wait(barrier, 2 + greetings)

    my_rows = pl.ds(pl.multiple_of(me * BLK, BLK), BLK)

    def first(c, d):
        v0, nv = CHUNKS[c]
        to = lax.rem(me + d, ND)
        return pltpu.make_async_remote_copy(
            src_ref=adj_hbm.at[:, pl.ds(v0, nv), pl.ds(pl.multiple_of(to * BLK, BLK), BLK)],
            dst_ref=gathered.at[d, :, pl.ds(v0, nv)],
            send_sem=send1.at[c, d], recv_sem=recv1.at[c, d],
            device_id={"inst": to}, device_id_type=MESH,
        )

    def second(c, d):
        v0, nv = CHUNKS[c]
        to = lax.rem(me + d, ND)
        return pltpu.make_async_remote_copy(
            src_ref=turned.at[d, :, pl.ds(v0, nv)],
            dst_ref=spectral.at[:, pl.ds(v0, nv), my_rows],
            send_sem=send2.at[c, d], recv_sem=recv2.at[c, d],
            device_id={"inst": to}, device_id_type=MESH,
        )

    def face_to(other):
        return pltpu.make_async_remote_copy(
            src_ref=payload, dst_ref=faces.at[sector],
            send_sem=face_send.at[other], recv_sem=face_recv.at[sector],
            device_id={"space": 2 * other + 1 - side}, device_id_type=MESH,
        )

    def face_from(other):
        return pltpu.make_async_remote_copy(
            src_ref=payload, dst_ref=faces.at[other],
            send_sem=face_send.at[other], recv_sem=face_recv.at[other],
            device_id={"space": 2 * other + 1 - side}, device_id_type=MESH,
        )

    def halo_to(i):
        return pltpu.make_async_remote_copy(
            src_ref=edges.at[i], dst_ref=halos.at[i],
            send_sem=halo_send.at[i], recv_sem=halo_recv.at[i],
            device_id=(next_id, prev_id)[i], device_id_type=MESH,
        )

    chunks = range(len(CHUNKS))

    def heard_of(i):
        pl.semaphore_wait(heard.at[i], 1)

    def signal(semaphore, device):
        pl.semaphore_signal(semaphore, inc=1, device_id=device, device_id_type=MESH)

    def tell(device, i):
        signal(heard.at[i], device)

    def unless_known(d):
        known = me == -1
        for late in KNOWN:
            if (late + d) % ND in KNOWN[late]:
                known = jnp.logical_or(known, me == late)
        pl.when(jnp.logical_not(known))(lambda: first(0, d).start())

    tell(down, 0)
    tell(up, 1)
    first(0, 1).start()
    first(0, ND - 1).start()
    for late in KNOWN:

        @pl.when(me == late)
        def send_known(late=late):
            for early in KNOWN[late]:
                first(0, (early - late) % ND).start()

    heard_of(0)
    tell(down, 2)
    unless_known(2)
    heard_of(1)
    tell(up, 3)
    unless_known(ND - 2)
    heard_of(2)
    tell(down, 4)
    unless_known(3)
    heard_of(3)
    unless_known(ND - 3)
    heard_of(4)
    unless_known(4)
    pl.when(jnp.logical_not(is_hub))(lambda: signal(column_in, at(x, 0, side)))
    for c in chunks[1:]:
        for d in ORDER:
            first(c, d).start()
    for copy in loads:
        copy.wait()

    wide = lax.broadcasted_iota(jnp.int32, (ROWS, LANES), 1)
    outward = coef[3]
    columns = jnp.zeros((ROWS, LANES), jnp.float32)
    for k in range(2 * NV):
        n, u = divmod(k, NV)
        columns = jnp.where(wide == k, pltpu.roll(outward * adj[n, u], k + 1, 1), columns)
        edges[0, k : k + 1, :] = coef[1, ROWS - 1 : ROWS, :] * adj[n, u, ROWS - 1 : ROWS, :]
        edges[1, k : k + 1, :] = coef[2, 0:1, :] * adj[n, u, 0:1, :]
    payload[...] = columns.T[0 : 2 * NV, :]

    pl.when(next_earlier)(lambda: halo_to(0).start())
    pl.when(prev_earlier)(lambda: halo_to(1).start())

    lane = lax.broadcasted_iota(jnp.int32, (BLK, LANES), 1)

    def stencil(step, carry):
        n = step // (ROWS // BLK)
        rows = pl.ds(pl.multiple_of(lax.rem(step, ROWS // BLK) * BLK, BLK), BLK)
        field = [adj[n, u, rows, :] for u in range(NV)]
        total = [base[n, v, rows, :] for v in range(NV)]
        for k in range(5):
            scale = coef[k, rows, :]
            q = [scale * f for f in field]
            for v in range(NV):
                mixed = mixing[k, 0, v] * q[0]
                for u in range(1, NV):
                    mixed = mixed + mixing[k, u, v] * q[u]
                if k == 0:
                    total[v] = total[v] + mixed
                elif k == 1:
                    ahead[n, v, rows, :] = mixed
                elif k == 2:
                    behind[n, v, rows, :] = mixed
                elif k == 3:
                    total[v] = total[v] + jnp.where(lane == 0, 0.0, pltpu.roll(mixed, 1, 1))
                else:
                    total[v] = total[v] + jnp.where(lane == LANES - 1, 0.0, pltpu.roll(mixed, LANES - 1, 1))
        for v in range(NV):
            base[n, v, rows, :] = total[v]
        return carry

    lax.fori_loop(0, 2 * (ROWS // BLK), stencil, 0)

    row = lax.broadcasted_iota(jnp.int32, (ROWS, LANES), 0)

    def moved(step, carry):
        n, v = step // NV, lax.rem(step, NV)
        down = jnp.where(row == 0, 0.0, pltpu.roll(ahead[n, v], 1, 0))
        up = jnp.where(row == ROWS - 1, 0.0, pltpu.roll(behind[n, v], ROWS - 1, 0))
        base[n, v] = base[n, v] + (down + up)
        return carry

    lax.fori_loop(0, 2 * NV, moved, 0)

    def report():
        pl.semaphore_wait(column_in, NZ - 1)
        pl.when(jnp.logical_not(is_chief))(lambda: signal(columns_in, at(0, 0, 1)))

    def spread():
        pl.semaphore_wait(columns_in, 2 * NX - 1)
        over_hubs(lambda device: signal(all_in, device))

    def send_faces():
        pl.when(jnp.logical_not(is_chief))(lambda: pl.semaphore_wait(all_in, 1))
        pl.when(is_hub)(lambda: over_column(lambda device: signal(all_in, device)))

        def send_face(other, carry):
            face_to(other).start()
            return carry

        lax.fori_loop(0, SECTORS, send_face, 0)

    pl.when(is_hub)(report)

    entries = spectral_entries()
    half = NI // 2

    def transform(c):
        v0, nv = CHUNKS[c]

        def body(step, carry):
            v = v0 + step // 2
            part = lax.rem(step, 2) * 8
            rows = pl.ds(pl.multiple_of(part, 8), 8)
            mine = pl.ds(pl.multiple_of(me * BLK + part, 8), 8)
            x = []
            for a in range(NI):
                slot, i = (-(a // 2)) % ND, a % 2
                x.append(adj[i, v, mine, :] if slot == 0 else gathered[slot, i, v, rows, :])
            plus = [x[a] + x[a + half] for a in range(half)]
            minus = [x[a] - x[a + half] for a in range(half)]
            for b in range(half):
                even, odd = None, None
                for a in range(half):
                    low, high = entries[(a - b) % NI], entries[(a + half - b) % NI]
                    even_term = np.float32(0.5 * (low + high)) * plus[a]
                    odd_term = np.float32(0.5 * (low - high)) * minus[a]
                    even = even_term if even is None else even + even_term
                    odd = odd_term if odd is None else odd + odd_term
                for n, value in ((b, even + odd), (b + half, even - odd)):
                    slot, j = n // 2, n % 2
                    if slot == 0:
                        spectral[j, v, mine, :] = value
                    else:
                        turned[slot, j, v, rows, :] = value
            return carry

        lax.fori_loop(0, 2 * nv, body, 0)

    for c in chunks:
        for d in ORDER:
            first(c, d).wait_recv()
        transform(c)
        to_first = lax.rem(ND - me, ND)
        if c:
            pl.when(to_first != 0)(lambda: second(c, to_first).start())
        for core, order in enumerate(((4, 5, 3, 6, 2, 7, 1), (7, 1, 6, 2, 5, 3, 4))):

            @pl.when(side == core)
            def send_back(c=c, order=order):
                for d in order:
                    if c:
                        pl.when(to_first != d)(lambda d=d: second(c, d).start())
                    else:
                        second(c, d).start()

        if c == 0:
            pl.when(is_chief)(spread)
            send_faces()

    def answer_next():
        halo_to(1).wait_recv()
        halo_to(0).start()

    def answer_prev():
        halo_to(0).wait_recv()
        halo_to(1).start()

    pl.when(jnp.logical_not(next_earlier))(answer_next)
    pl.when(jnp.logical_not(prev_earlier))(answer_prev)

    pl.when(next_earlier)(lambda: halo_to(1).wait_recv())
    pl.when(prev_earlier)(lambda: halo_to(0).wait_recv())

    def take_face(other, carry):
        face_from(other).wait_recv()
        return carry

    lax.fori_loop(0, SECTORS, take_face, 0)

    thin = lax.broadcasted_iota(jnp.int32, (2 * NV, LANES), 1) // FB
    mixed = []
    for n in range(2):
        rows = jnp.zeros((2 * NV, LANES), jnp.float32)
        for b in range(NB):
            block = partner[n, NB * p + b]
            face, kind = faces[block // (2 * NB)], lax.rem(block, NB)
            for turn in range(NB):
                here = jnp.logical_and(thin == b, kind == (b - turn) % NB)
                rows = jnp.where(here, pltpu.roll(face, turn * FB, 1) if turn else face, rows)
        for v in range(NV):
            mixed.append(sum(mixing[3, u, v] * rows[n * NV + u : n * NV + u + 1, :] for u in range(NV)))
    mixed = jnp.concatenate(mixed + [jnp.zeros((LANES - 2 * NV, LANES), jnp.float32)], axis=0).T
    for k in range(2 * NV):
        n, v = divmod(k, NV)
        column = pltpu.roll(mixed, LANES - 1 - k, 1)
        base[n, v] = base[n, v] + jnp.where(wide == LANES - 1, column, 0.0)
        first_row = sum(mixing[1, u, v] * halos[0, n * NV + u : n * NV + u + 1, :] for u in range(NV))
        last_row = sum(mixing[2, u, v] * halos[1, n * NV + u : n * NV + u + 1, :] for u in range(NV))
        base[n, v, 0:1, :] = base[n, v, 0:1, :] + first_row
        base[n, v, ROWS - 1 : ROWS, :] = base[n, v, ROWS - 1 : ROWS, :] + last_row

    for c in chunks:
        v0, nv = CHUNKS[c]
        for d in ORDER:
            second(c, d).wait_recv()

        def finish(step, carry, v0=v0):
            v = v0 + step // 2
            n = lax.rem(step, 2)
            out[n, v] = base[n, v] + (SPIN_RATE * vol[...]) * spectral[n, v]
            return carry

        lax.fori_loop(0, 2 * nv, finish, 0)
    for c in chunks:
        for d in ORDER:
            first(c, d).wait_send()
            second(c, d).wait_send()

    def sent_face(other, carry):
        face_to(other).wait_send()
        return carry

    lax.fori_loop(0, SECTORS, sent_face, 0)
    for i in range(2):
        halo_to(i).wait_send()


def local(adjoint, source, coefficient, volume, mixing, face_partner):
    f32 = jnp.float32
    hbm = pl.BlockSpec(memory_space=pltpu.HBM)
    shard = (2, NV, ROWS, LANES)
    nc = len(CHUNKS)
    given = (adjoint, source, coefficient, volume, mixing, face_partner)
    operands = [pltpu.with_memory_space_constraint(t, pltpu.HBM) for t in given]
    return pl.pallas_call(
        main_kernel,
        out_shape=jax.ShapeDtypeStruct(shard, f32),
        in_specs=[hbm] * 6,
        out_specs=pl.BlockSpec(memory_space=pltpu.VMEM),
        scratch_shapes=[
            pltpu.VMEM(shard, f32), pltpu.VMEM(shard, f32),
            pltpu.VMEM((5, ROWS, LANES), f32), pltpu.VMEM((ROWS, LANES), f32),
            pltpu.VMEM(shard, f32), pltpu.VMEM(shard, f32),
            pltpu.VMEM((ND, 2, NV, BLK, LANES), f32), pltpu.VMEM((ND, 2, NV, BLK, LANES), f32),
            pltpu.VMEM(shard, f32),
            pltpu.VMEM((2 * NV, LANES), f32), pltpu.VMEM((SECTORS, 2 * NV, LANES), f32),
            pltpu.VMEM((2, 2 * NV, LANES), f32), pltpu.VMEM((2, 2 * NV, LANES), f32),
            pltpu.SMEM((5, NV, NV), f32), pltpu.SMEM((2, SECTORS * 2 * NB), jnp.int32),
            pltpu.SemaphoreType.DMA((6,)),
            pltpu.SemaphoreType.DMA((nc, ND)), pltpu.SemaphoreType.DMA((nc, ND)),
            pltpu.SemaphoreType.DMA((nc, ND)), pltpu.SemaphoreType.DMA((nc, ND)),
            pltpu.SemaphoreType.DMA((SECTORS,)), pltpu.SemaphoreType.DMA((SECTORS,)),
            pltpu.SemaphoreType.DMA((2,)), pltpu.SemaphoreType.DMA((2,)),
            pltpu.SemaphoreType.REGULAR((5,)),
            pltpu.SemaphoreType.REGULAR, pltpu.SemaphoreType.REGULAR, pltpu.SemaphoreType.REGULAR,
        ],
        compiler_params=pltpu.CompilerParams(
            collective_id=0, has_side_effects=True, vmem_limit_bytes=VMEM_LIMIT
        ),
        cost_estimate=pl.CostEstimate(flops=20_000_000, bytes_accessed=60_000_000, transcendentals=0),
        name="residual",
    )(*operands)


def solution(mesh):
    in_specs = (
        P("inst", None, "space", None),
        P("inst", None, "space", None),
        P(None, "space", None),
        P("space", None),
        P(),
        P("inst", None),
    )
    out_specs = P("inst", None, "space", None)
    return jax.shard_map(local, mesh=mesh, in_specs=in_specs, out_specs=out_specs, check_vma=False)
```

```python
import functools

import numpy as np

import jax
import jax.numpy as jnp
from jax import lax
from jax.experimental import pallas as pl
from jax.experimental.pallas import tpu as pltpu
from jax.sharding import PartitionSpec as P

MESH = pl.DeviceIdType.MESH
NI = 16
ND = 8
NX = 4
NZ = 8
SECTORS = NX * NZ
SPACE = 2 * SECTORS
NV = 5
NB = 4
FB = 32
BLK = 16
ROWS = 128
LANES = 128
SPIN_RATE = 0.75
KNOWN = {4: (0, 1, 2), 5: (0, 1), 6: (0, 1), 7: (1,), 3: (0,)}
CHUNKS = ((0, 3), (3, 2))
ORDER = (4, 3, 5, 2, 6, 1, 7)
VMEM_LIMIT = 16 * 1024 * 1024


def spectral_entries():
    offset = np.arange(1, NI)
    angle = np.pi * offset / NI
    entries = 0.5 * np.where(offset % 2 == 0, 1.0, -1.0) * np.cos(angle) / np.sin(angle)
    return np.concatenate([[0.0], entries])


def main_kernel(
    adj_hbm, src_hbm, coef_hbm, vol_hbm, mixing_hbm, partner_hbm, out,
    adj, base, coef, vol, ahead, behind, gathered, turned, spectral, payload, faces, edges, halos,
    mixing, partner,
    load_sem, send1, recv1, send2, recv2, face_send, face_recv, halo_send, halo_recv, heard, column_in, columns_in, all_in,
):
    me = lax.axis_index("inst")
    p = lax.axis_index("space")
    side = lax.rem(p, 2)
    z, x = lax.rem(p // 2, NZ), p // (2 * NZ)
    sector = x * NZ + z
    is_hub = z == 0
    is_chief = jnp.logical_and(is_hub, jnp.logical_and(x == 0, side == 1))
    next_earlier, prev_earlier = z == NZ - 1, z != 0
    next_id = {"space": lax.rem(p + 2, SPACE)}
    prev_id = {"space": lax.rem(p + SPACE - 2, SPACE)}

    def at(x, z, side):
        return {"space": 2 * (x * NZ + z) + side}

    def over_hubs(act):
        for other in range(NX):
            if other:
                act(at(other, 0, 1))
            act(at(other, 0, 0))

    def over_column(act):
        for other in range(1, NZ):
            act(at(x, other, side))

    barrier = pltpu.get_barrier_semaphore()

    def greet(device):
        pl.semaphore_signal(barrier, inc=1, device_id=device, device_id_type=MESH)

    up, down = {"inst": lax.rem(me + 1, ND)}, {"inst": lax.rem(me + ND - 1, ND)}
    greet(up)
    greet(down)
    for early in range(ND):
        later = [late for late in KNOWN if early in KNOWN[late]]
        if later:

            @pl.when(me == early)
            def greet_later(later=later):
                for late in later:
                    greet({"inst": late})


    pl.when(is_chief)(lambda: over_hubs(greet))
    pl.when(is_hub)(lambda: over_column(greet))
    pl.when(jnp.logical_not(next_earlier))(lambda: greet(next_id))
    pl.when(jnp.logical_not(prev_earlier))(lambda: greet(prev_id))
    loads = [
        pltpu.make_async_copy(s, t, load_sem.at[i])
        for i, (s, t) in enumerate((
            (adj_hbm, adj), (coef_hbm, coef), (src_hbm, base), (vol_hbm, vol),
            (mixing_hbm, mixing), (partner_hbm, partner),
        ))
    ]
    for copy in loads:
        copy.start()
    greetings = jnp.where(is_hub, 1 - is_chief.astype(jnp.int32), 2 + next_earlier.astype(jnp.int32))
    for late in KNOWN:
        greetings = greetings + jnp.where(me == late, len(KNOWN[late]), 0)
    pl.semaphore_wait(barrier, 2 + greetings)

    my_rows = pl.ds(pl.multiple_of(me * BLK, BLK), BLK)

    def first(c, d):
        v0, nv = CHUNKS[c]
        to = lax.rem(me + d, ND)
        return pltpu.make_async_remote_copy(
            src_ref=adj_hbm.at[:, pl.ds(v0, nv), pl.ds(pl.multiple_of(to * BLK, BLK), BLK)],
            dst_ref=gathered.at[d, :, pl.ds(v0, nv)],
            send_sem=send1.at[c, d], recv_sem=recv1.at[c, d],
            device_id={"inst": to}, device_id_type=MESH,
        )

    def second(c, d):
        v0, nv = CHUNKS[c]
        to = lax.rem(me + d, ND)
        return pltpu.make_async_remote_copy(
            src_ref=turned.at[d, :, pl.ds(v0, nv)],
            dst_ref=spectral.at[:, pl.ds(v0, nv), my_rows],
            send_sem=send2.at[c, d], recv_sem=recv2.at[c, d],
            device_id={"inst": to}, device_id_type=MESH,
        )

    def face_to(other):
        return pltpu.make_async_remote_copy(
            src_ref=payload, dst_ref=faces.at[sector],
            send_sem=face_send.at[other], recv_sem=face_recv.at[sector],
            device_id={"space": 2 * other + 1 - side}, device_id_type=MESH,
        )

    def face_from(other):
        return pltpu.make_async_remote_copy(
            src_ref=payload, dst_ref=faces.at[other],
            send_sem=face_send.at[other], recv_sem=face_recv.at[other],
            device_id={"space": 2 * other + 1 - side}, device_id_type=MESH,
        )

    def halo_to(i):
        return pltpu.make_async_remote_copy(
            src_ref=edges.at[i], dst_ref=halos.at[i],
            send_sem=halo_send.at[i], recv_sem=halo_recv.at[i],
            device_id=(next_id, prev_id)[i], device_id_type=MESH,
        )

    chunks = range(len(CHUNKS))

    def heard_of(i):
        pl.semaphore_wait(heard.at[i], 1)

    def signal(semaphore, device):
        pl.semaphore_signal(semaphore, inc=1, device_id=device, device_id_type=MESH)

    def tell(device, i):
        signal(heard.at[i], device)

    def unless_known(d):
        known = me == -1
        for late in KNOWN:
            if (late + d) % ND in KNOWN[late]:
                known = jnp.logical_or(known, me == late)
        pl.when(jnp.logical_not(known))(lambda: first(0, d).start())

    tell(down, 0)
    tell(up, 1)
    first(0, 1).start()
    first(0, ND - 1).start()
    for late in KNOWN:

        @pl.when(me == late)
        def send_known(late=late):
            for early in KNOWN[late]:
                first(0, (early - late) % ND).start()

    heard_of(0)
    tell(down, 2)
    unless_known(2)
    heard_of(1)
    tell(up, 3)
    unless_known(ND - 2)
    heard_of(2)
    tell(down, 4)
    unless_known(3)
    heard_of(3)
    unless_known(ND - 3)
    heard_of(4)
    unless_known(4)
    pl.when(jnp.logical_not(is_hub))(lambda: signal(column_in, at(x, 0, side)))
    for c in chunks[1:]:
        for d in ORDER:
            first(c, d).start()
    for copy in loads:
        copy.wait()

    wide = lax.broadcasted_iota(jnp.int32, (ROWS, LANES), 1)
    outward = coef[3]
    columns = jnp.zeros((ROWS, LANES), jnp.float32)
    for k in range(2 * NV):
        n, u = divmod(k, NV)
        columns = jnp.where(wide == k, pltpu.roll(outward * adj[n, u], k + 1, 1), columns)
        edges[0, k : k + 1, :] = coef[1, ROWS - 1 : ROWS, :] * adj[n, u, ROWS - 1 : ROWS, :]
        edges[1, k : k + 1, :] = coef[2, 0:1, :] * adj[n, u, 0:1, :]
    payload[...] = columns.T[0 : 2 * NV, :]

    pl.when(next_earlier)(lambda: halo_to(0).start())
    pl.when(prev_earlier)(lambda: halo_to(1).start())

    lane = lax.broadcasted_iota(jnp.int32, (BLK, LANES), 1)

    def stencil(step, carry):
        n = step // (ROWS // BLK)
        rows = pl.ds(pl.multiple_of(lax.rem(step, ROWS // BLK) * BLK, BLK), BLK)
        field = [adj[n, u, rows, :] for u in range(NV)]
        total = [base[n, v, rows, :] for v in range(NV)]
        for k in range(5):
            scale = coef[k, rows, :]
            q = [scale * f for f in field]
            for v in range(NV):
                mixed = mixing[k, 0, v] * q[0]
                for u in range(1, NV):
                    mixed = mixed + mixing[k, u, v] * q[u]
                if k == 0:
                    total[v] = total[v] + mixed
                elif k == 1:
                    ahead[n, v, rows, :] = mixed
                elif k == 2:
                    behind[n, v, rows, :] = mixed
                elif k == 3:
                    total[v] = total[v] + jnp.where(lane == 0, 0.0, pltpu.roll(mixed, 1, 1))
                else:
                    total[v] = total[v] + jnp.where(lane == LANES - 1, 0.0, pltpu.roll(mixed, LANES - 1, 1))
        for v in range(NV):
            base[n, v, rows, :] = total[v]
        return carry

    lax.fori_loop(0, 2 * (ROWS // BLK), stencil, 0)

    row = lax.broadcasted_iota(jnp.int32, (ROWS, LANES), 0)

    def moved(step, carry):
        n, v = step // NV, lax.rem(step, NV)
        down = jnp.where(row == 0, 0.0, pltpu.roll(ahead[n, v], 1, 0))
        up = jnp.where(row == ROWS - 1, 0.0, pltpu.roll(behind[n, v], ROWS - 1, 0))
        base[n, v] = base[n, v] + (down + up)
        return carry

    lax.fori_loop(0, 2 * NV, moved, 0)

    def report():
        pl.semaphore_wait(column_in, NZ - 1)
        pl.when(jnp.logical_not(is_chief))(lambda: signal(columns_in, at(0, 0, 1)))

    def spread():
        pl.semaphore_wait(columns_in, 2 * NX - 1)
        over_hubs(lambda device: signal(all_in, device))

    def send_faces():
        pl.when(jnp.logical_not(is_chief))(lambda: pl.semaphore_wait(all_in, 1))
        pl.when(is_hub)(lambda: over_column(lambda device: signal(all_in, device)))

        def send_face(other, carry):
            face_to(other).start()
            return carry

        lax.fori_loop(0, SECTORS, send_face, 0)

    pl.when(is_hub)(report)

    entries = spectral_entries()
    half = NI // 2

    def transform(c):
        v0, nv = CHUNKS[c]

        def body(step, carry):
            v = v0 + step // 2
            part = lax.rem(step, 2) * 8
            rows = pl.ds(pl.multiple_of(part, 8), 8)
            mine = pl.ds(pl.multiple_of(me * BLK + part, 8), 8)
            x = []
            for a in range(NI):
                slot, i = (-(a // 2)) % ND, a % 2
                x.append(adj[i, v, mine, :] if slot == 0 else gathered[slot, i, v, rows, :])
            plus = [x[a] + x[a + half] for a in range(half)]
            minus = [x[a] - x[a + half] for a in range(half)]
            for b in range(half):
                even, odd = None, None
                for a in range(half):
                    low, high = entries[(a - b) % NI], entries[(a + half - b) % NI]
                    even_term = np.float32(0.5 * (low + high)) * plus[a]
                    odd_term = np.float32(0.5 * (low - high)) * minus[a]
                    even = even_term if even is None else even + even_term
                    odd = odd_term if odd is None else odd + odd_term
                for n, value in ((b, even + odd), (b + half, even - odd)):
                    slot, j = n // 2, n % 2
                    if slot == 0:
                        spectral[j, v, mine, :] = value
                    else:
                        turned[slot, j, v, rows, :] = value
            return carry

        lax.fori_loop(0, 2 * nv, body, 0)

    for c in chunks:
        for d in ORDER:
            first(c, d).wait_recv()
        transform(c)
        to_first = lax.rem(ND - me, ND)
        if c:
            pl.when(jnp.logical_and(side == 0, to_first != 0))(lambda: second(c, to_first).start())
        for core, order in enumerate(((4, 5, 3, 6, 2, 7, 1), (7, 1, 6, 2, 5, 3, 4))):

            @pl.when(side == core)
            def send_back(c=c, core=core, order=order):
                for d in order:
                    if c and core == 0:
                        pl.when(to_first != d)(lambda d=d: second(c, d).start())
                    else:
                        second(c, d).start()

        if c == 0:
            pl.when(is_chief)(spread)
            send_faces()

    def answer_next():
        halo_to(1).wait_recv()
        halo_to(0).start()

    def answer_prev():
        halo_to(0).wait_recv()
        halo_to(1).start()

    pl.when(jnp.logical_not(next_earlier))(answer_next)
    pl.when(jnp.logical_not(prev_earlier))(answer_prev)

    pl.when(next_earlier)(lambda: halo_to(1).wait_recv())
    pl.when(prev_earlier)(lambda: halo_to(0).wait_recv())

    def take_face(other, carry):
        face_from(other).wait_recv()
        return carry

    lax.fori_loop(0, SECTORS, take_face, 0)

    thin = lax.broadcasted_iota(jnp.int32, (2 * NV, LANES), 1) // FB
    mixed = []
    for n in range(2):
        rows = jnp.zeros((2 * NV, LANES), jnp.float32)
        for b in range(NB):
            block = partner[n, NB * p + b]
            face, kind = faces[block // (2 * NB)], lax.rem(block, NB)
            for turn in range(NB):
                here = jnp.logical_and(thin == b, kind == (b - turn) % NB)
                rows = jnp.where(here, pltpu.roll(face, turn * FB, 1) if turn else face, rows)
        for v in range(NV):
            mixed.append(sum(mixing[3, u, v] * rows[n * NV + u : n * NV + u + 1, :] for u in range(NV)))
    mixed = jnp.concatenate(mixed + [jnp.zeros((LANES - 2 * NV, LANES), jnp.float32)], axis=0).T
    for k in range(2 * NV):
        n, v = divmod(k, NV)
        column = pltpu.roll(mixed, LANES - 1 - k, 1)
        base[n, v] = base[n, v] + jnp.where(wide == LANES - 1, column, 0.0)
        first_row = sum(mixing[1, u, v] * halos[0, n * NV + u : n * NV + u + 1, :] for u in range(NV))
        last_row = sum(mixing[2, u, v] * halos[1, n * NV + u : n * NV + u + 1, :] for u in range(NV))
        base[n, v, 0:1, :] = base[n, v, 0:1, :] + first_row
        base[n, v, ROWS - 1 : ROWS, :] = base[n, v, ROWS - 1 : ROWS, :] + last_row

    for c in chunks:
        v0, nv = CHUNKS[c]
        for d in ORDER:
            second(c, d).wait_recv()

        def finish(step, carry, v0=v0):
            v = v0 + step // 2
            n = lax.rem(step, 2)
            out[n, v] = base[n, v] + (SPIN_RATE * vol[...]) * spectral[n, v]
            return carry

        lax.fori_loop(0, 2 * nv, finish, 0)
    for c in chunks:
        for d in ORDER:
            first(c, d).wait_send()
            second(c, d).wait_send()

    def sent_face(other, carry):
        face_to(other).wait_send()
        return carry

    lax.fori_loop(0, SECTORS, sent_face, 0)
    for i in range(2):
        halo_to(i).wait_send()


def local(adjoint, source, coefficient, volume, mixing, face_partner):
    f32 = jnp.float32
    hbm = pl.BlockSpec(memory_space=pltpu.HBM)
    shard = (2, NV, ROWS, LANES)
    nc = len(CHUNKS)
    given = (adjoint, source, coefficient, volume, mixing, face_partner)
    operands = [pltpu.with_memory_space_constraint(t, pltpu.HBM) for t in given]
    return pl.pallas_call(
        main_kernel,
        out_shape=jax.ShapeDtypeStruct(shard, f32),
        in_specs=[hbm] * 6,
        out_specs=pl.BlockSpec(memory_space=pltpu.VMEM),
        scratch_shapes=[
            pltpu.VMEM(shard, f32), pltpu.VMEM(shard, f32),
            pltpu.VMEM((5, ROWS, LANES), f32), pltpu.VMEM((ROWS, LANES), f32),
            pltpu.VMEM(shard, f32), pltpu.VMEM(shard, f32),
            pltpu.VMEM((ND, 2, NV, BLK, LANES), f32), pltpu.VMEM((ND, 2, NV, BLK, LANES), f32),
            pltpu.VMEM(shard, f32),
            pltpu.VMEM((2 * NV, LANES), f32), pltpu.VMEM((SECTORS, 2 * NV, LANES), f32),
            pltpu.VMEM((2, 2 * NV, LANES), f32), pltpu.VMEM((2, 2 * NV, LANES), f32),
            pltpu.SMEM((5, NV, NV), f32), pltpu.SMEM((2, SECTORS * 2 * NB), jnp.int32),
            pltpu.SemaphoreType.DMA((6,)),
            pltpu.SemaphoreType.DMA((nc, ND)), pltpu.SemaphoreType.DMA((nc, ND)),
            pltpu.SemaphoreType.DMA((nc, ND)), pltpu.SemaphoreType.DMA((nc, ND)),
            pltpu.SemaphoreType.DMA((SECTORS,)), pltpu.SemaphoreType.DMA((SECTORS,)),
            pltpu.SemaphoreType.DMA((2,)), pltpu.SemaphoreType.DMA((2,)),
            pltpu.SemaphoreType.REGULAR((5,)),
            pltpu.SemaphoreType.REGULAR, pltpu.SemaphoreType.REGULAR, pltpu.SemaphoreType.REGULAR,
        ],
        compiler_params=pltpu.CompilerParams(
            collective_id=0, has_side_effects=True, vmem_limit_bytes=VMEM_LIMIT
        ),
        cost_estimate=pl.CostEstimate(flops=20_000_000, bytes_accessed=60_000_000, transcendentals=0),
        name="residual",
    )(*operands)


def solution(mesh):
    in_specs = (
        P("inst", None, "space", None),
        P("inst", None, "space", None),
        P(None, "space", None),
        P("space", None),
        P(),
        P("inst", None),
    )
    out_specs = P("inst", None, "space", None)
    return jax.shard_map(local, mesh=mesh, in_specs=in_specs, out_specs=out_specs, check_vma=False)
```
